512 devices in a mesh: dp: 32 (over x, y, core), seq: 16 (over z).
Axes of the slice: x: 4, y: 4, z: 16, core: 2. Of those that a mesh axis runs over, the one named last changes fastest.
Arguments:
- tile_tokens: bfloat16 [32, 512, 3200], P('dp', 'seq'), may hold values from -6 to 6
- proj_weight: bfloat16 [3200, 8192], P('dp', 'seq')
- text_hidden: bfloat16 [32, 2048, 8192], P('dp', 'seq'), may hold values from -6 to 6
- cotangent: bfloat16 [32, 2048, 8192], P('dp', 'seq'), may hold values from -1.1953125 to 1.1953125
- norm_gain: float32 [8192], replicated, may hold values from 0.25 to 1.75
- placeholders: int32 [32, 512], P('dp'), may hold values from 0 to 2047, as said below
- bucket_levels: int32 [32, 16, 3200], P('dp', 'seq'), may hold values from 2 to 16
- row_draws: float32 [32, 16, 3200], P('dp', 'seq'), may hold values from 0 to 1
- column_draws: float32 [32, 8192], P('dp', 'seq'), may hold values from 0 to 1
Outputs:
- weight_grad: float32 [3200, 8192], P('dp', 'seq')
- gain_grad: float32 [8192], replicated
The draws below stay inside these ranges and needn't reach their ends.
Inputs may be any that keep to these rules, and one draw needn't show every extreme that they name: Each row is strictly increasing. Among the positions of one device's block of 128 positions stand at most 48 placeholders, and in every row some block holds exactly 48.
All inputs are finite; a program needn't handle non-finite values.
Results may differ from the reference program's by a relative error of at most 0.014.
Values may be sent and summed in bfloat16 or wider, within the bound.
A program may use at most 64 MiB of HBM per device.

```python
import math
import jax
import jax.numpy as jnp
from jax import lax

VD = 3200
D = 8192
IMG_DEV = 32
TOK_DEV = 128
IMG = 512
TOKENS = 2048
N_DP = 32
N_SEQ = 16


def draw_proj_weight(key, part):
    group_width = max(D // 64, 1)
    group_total = D // group_width
    first_key, second_key = jax.random.split(jax.random.fold_in(key, 11))
    logs = jax.random.uniform(second_key, (group_total,), jnp.float32, -1.15, 1.15)
    column_scale = jnp.repeat(jnp.exp(logs), group_width)
    base = jax.random.normal(first_key, (VD, D), jnp.float32)
    return (base * column_scale[None, :] / math.sqrt(VD)).astype(jnp.bfloat16)


def placeholder_list(key):
    owner_total = TOKENS // TOK_DEV
    half_extra = IMG_DEV // 2
    order_key, amount_key, choose_key = jax.random.split(key, 3)
    order = jax.random.permutation(order_key, owner_total)
    amounts = jax.random.randint(amount_key, (owner_total // 2,), 0, half_extra + 1)
    amounts = amounts.at[0].set(half_extra)
    paired = jnp.stack([amounts, -amounts], axis=1).reshape(-1)
    delta = jnp.zeros((owner_total,), jnp.int32).at[order].set(paired.astype(jnp.int32))
    counts = IMG_DEV + delta
    owner_keys = jax.random.split(choose_key, owner_total)
    ranking = jax.vmap(lambda one_key: jax.random.permutation(one_key, TOK_DEV))(owner_keys)
    chosen = (ranking < counts[:, None]).reshape(-1)
    sort_keys = jnp.where(chosen, 0, 1) * TOKENS + jnp.arange(TOKENS, dtype=jnp.int32)
    return jnp.argsort(sort_keys)[:IMG].astype(jnp.int32)


def draw_placeholders(key, part):
    replica_keys = jax.random.split(jax.random.fold_in(key, 23), N_DP)
    return jax.vmap(placeholder_list)(replica_keys)


def set_ends(array, rng, low, largest):
    index_at = [jax.random.randint(jax.random.fold_in(rng, axis), (), 0, length) for axis, length in enumerate(array.shape)]
    main_axis = array.shape.index(max(array.shape))
    beside = index_at[:main_axis] + [(index_at[main_axis] + 1) % array.shape[main_axis]] + index_at[main_axis + 1:]
    return array.at[tuple(index_at)].set(low).at[tuple(beside)].set(largest)


def strengthened(entries, rng, source, target, shards_of, factor):
    owner, partner = [(jnp.arange(entries.shape[position]) // (entries.shape[position] // shards_of)).reshape([-1 if axis == position else 1 for axis in range(entries.ndim)]) for position in (source, target)]
    chosen = jax.random.permutation(rng, shards_of)[partner]
    strong = (owner == chosen) | (owner == (partner + shards_of // 2) % shards_of)
    return jnp.where(strong, factor * entries, entries)


def block_levels(rng, extent, pieces, least, largest):
    loudness = 1.0
    for position, shards_of in pieces:
        draws = jax.random.uniform(jax.random.fold_in(jax.random.fold_in(rng, 6), position), (shards_of,), jnp.float32, least / len(pieces), largest / len(pieces))
        loudness = loudness * jnp.repeat(jnp.exp(draws), extent[position] // shards_of).reshape((-1,) + (1,) * (len(extent) - 1 - position))
    return loudness


def noise(rng, dims, spread, reach, pieces=(), kind=jnp.bfloat16):
    array = jax.random.normal(rng, dims, jnp.float32) * spread
    if len(pieces) > 0:
        array = block_levels(rng, dims, pieces, -0.22, 0.18) * array
    return jnp.clip(array, min=-reach, max=reach).astype(kind)


def bell_draw_with(own_key, dims, deviation, reach, shards, heavy, held_as=jnp.bfloat16):
    values = deviation * jax.random.normal(own_key, dims, jnp.float32)
    if shards:
        values = values * block_levels(own_key, dims, shards, -0.22, 0.18)
    return jnp.clip(strengthened(values, jax.random.fold_in(own_key, 3), *heavy), -reach, reach).astype(held_as)


def setup_inputs(seed: int = 0) -> dict:
    keys = jax.random.split(jax.random.key(seed), 10)
    return {
        "tile_tokens": bell_draw_with(keys[0], (N_DP, IMG, VD), 1.0, 6.0, ((0, 32), (1, 16)), (0, 2, 32, 2.75)),
        "proj_weight": draw_proj_weight(jax.random.fold_in(keys[9], 71), 0),
        "text_hidden": noise(keys[2], (N_DP, TOKENS, D), 1.0, 6.0, ((0, 32), (1, 16))),
        "cotangent": noise(keys[3], (N_DP, TOKENS, D), 0.2, 1.1953125, ((0, 32), (1, 16))),
        "norm_gain": jnp.clip(1.0 + 0.15 * jax.random.normal(keys[4], (D,), jnp.float32), 0.25, 1.75),
        "placeholders": draw_placeholders(jax.random.fold_in(keys[9], 71), 0),
        "bucket_levels": set_ends(jax.random.randint(keys[6], (N_DP, N_SEQ, VD), 2, 17), jax.random.fold_in(keys[6], 1), 2, 16).astype(jnp.int32),
        "row_draws": jnp.clip(1.0 * jax.random.uniform(keys[7], (N_DP, N_SEQ, VD), jnp.float32) ** block_levels(keys[7], (N_DP, N_SEQ, VD), ((0, 32), (1, 16)), -0.2, 0.2), 0.0, 1.0),
        "column_draws": jnp.clip(1.0 * jax.random.uniform(keys[8], (N_DP, D), jnp.float32) ** block_levels(keys[8], (N_DP, D), ((0, 32), (1, 16)), -0.2, 0.2), 0.0, 1.0),
    }


EPSILON = 1e-06

def quantize(gradient, levels_now, rows_now, columns_now):
    buckets = levels_now.shape[0]
    grouped = gradient.reshape(gradient.shape[0], buckets, -1)
    bucket_norm = jnp.sqrt(lax.optimization_barrier(jnp.sum(grouped * grouped, axis=2, keepdims=True)) + EPSILON)
    step_count = jnp.transpose(levels_now).astype(jnp.float32)[:, :, None]
    offset = 0.25 + 0.25 * (jnp.transpose(rows_now)[:, :, None] + columns_now.reshape(buckets, -1)[None, :, :])
    ratio = jnp.abs(grouped) / bucket_norm * step_count
    lower = jnp.floor(ratio)
    quantum = lower + jnp.clip(2.0 * (ratio - lower - offset) + 0.5, 0.0, 1.0)
    return (jnp.sign(grouped) * bucket_norm * quantum / step_count).reshape(gradient.shape)

def reference(tile_tokens, proj_weight, text_hidden, cotangent, norm_gain, placeholders, bucket_levels, row_draws, column_draws):

    def replica(running, inputs):
        weight_sum, gain_sum = running
        tile_rows, text_rows, cot_rows, places, levels_now, rows_now, columns_now = inputs
        embedded = jnp.dot(tile_rows, proj_weight, preferred_element_type=jnp.float32).astype(jnp.bfloat16)
        image_marks = jnp.zeros((TOKENS,), jnp.int32).at[places].set(1)
        image_ranks = jnp.clip(jnp.cumsum(image_marks) - image_marks, 0, IMG - 1).astype(jnp.int32)
        hidden = jnp.where(image_marks[:, None] == 1, jnp.take(embedded, image_ranks, axis=0), text_rows)
        hidden_f = hidden.astype(jnp.float32)
        inverse = lax.rsqrt(lax.optimization_barrier(jnp.mean(hidden_f * hidden_f, axis=1, keepdims=True)) + EPSILON)
        normed = hidden_f * inverse
        cot_float = cot_rows.astype(jnp.float32)
        grad_in = cot_float * norm_gain[None, :]
        hidden_grad = ((grad_in - normed * lax.optimization_barrier(jnp.mean(grad_in * normed, axis=1, keepdims=True))) * inverse).astype(jnp.bfloat16)
        emb_grad = jnp.take(hidden_grad, places, axis=0)
        gradient = lax.dot_general(tile_rows, emb_grad, (((0,), (0,)), ((), ())), preferred_element_type=jnp.float32)
        quantized = quantize(gradient, levels_now, rows_now, columns_now)
        rounded = lax.optimization_barrier(quantized.astype(jnp.bfloat16)).astype(jnp.float32)
        return ((weight_sum + rounded, gain_sum + lax.optimization_barrier(jnp.sum(cot_float * normed, axis=0))), None)
    initial = (jnp.zeros((VD, D), jnp.float32), jnp.zeros((D,), jnp.float32))
    inputs = (tile_tokens, text_hidden, cotangent, placeholders, bucket_levels, row_draws, column_draws)
    (weight_sum, gain_sum), unused = lax.scan(replica, initial, inputs)
    return (weight_sum / N_DP, gain_sum / N_DP)
```

```python
import functools

import jax
import jax.numpy as jnp
from jax import lax
from jax.experimental import pallas as pl
from jax.experimental.pallas import tpu as pltpu
from jax.sharding import Mesh
from jax.sharding import PartitionSpec as P

DP = ("dp_0", "dp_1", "dp_2")
MESH = pl.DeviceIdType.MESH
EPSILON = 1e-06
SLOTS = 48
GROUP = 4
F32 = jnp.float32
BF16 = jnp.bfloat16


def up(n, m):
    return -(-n // m) * m


def dot(a, b, dims=((1,), (0,))):
    return lax.dot_general(a, b, (dims, ((), ())), preferred_element_type=F32)


def iota(shape, axis):
    return lax.broadcasted_iota(jnp.int32, shape, axis)


def one_where(condition):
    return jnp.where(condition, 1.0, 0.0).astype(BF16)


def kernel(
    sizes,
    tile, w_own, cot, gain, places, levels, row_draws, column_draws, text_hbm,
    out, gain_out,
    tbuf, t_t, wbuf, wfull, text, outb, inb, emb, eg, icot, picks, sm_c, smb, marks, gacc,
    gz, gz_in, g_core, g_x, g_y, meta, qq, from_core, s_a, s_b, r_a, r_b, t_a, t_b, u_a, u_b, fown, f_in,
    text_sem, ag_s, ag_r, wx_s, wx_r, wy_s, wy_r, wc_s, wc_r, a2a_s, a2a_r, sm_s, sm_r, gz_s, gz_r,
    gc_s, gc_r, gx_s, gx_r, gy_s, gy_r, gf_s, gf_r, qc_s, qc_r,
    xa_s, xa_r, ya_s, ya_r, yb_s, yb_r, xb_s, xb_r, f_s, f_r,
):
    nx, ny, nz = sizes
    rows = w_own.shape[0]
    own_rows = t_t.shape[0] // (nx * ny * 2)
    img_dev, vd = tile.shape
    half_rows = img_dev // 2
    img = tbuf.shape[0]
    tok, d = cot.shape
    cols = w_own.shape[1]
    win = qq.shape[2]
    hc = cols // 2
    qc = cols // 4
    h = nz // 2
    mx, my, mc, mz = (lax.axis_index(a) for a in ("dp_0", "dp_1", "dp_2", "seq"))
    oc = 1 - mc

    def z_peer(k):
        return {"seq": lax.rem(mz + k, nz)}

    def z_source(k):
        return lax.rem(mz + nz - k, nz)

    def x_peer(k):
        return lax.rem(mx + k, nx)

    def y_peer(k):
        return lax.rem(my + k, ny)

    def x_source(k):
        return lax.rem(mx + nx - k, nx)

    def y_source(k):
        return lax.rem(my + ny - k, ny)

    def remote(src, dst, send, recv, where):
        return pltpu.make_async_remote_copy(
            src_ref=src, dst_ref=dst, send_sem=send, recv_sem=recv, device_id=where, device_id_type=MESH
        )

    text_copy = pltpu.make_async_copy(text_hbm, text, text_sem)
    text_copy.start()

    barrier = pltpu.get_barrier_semaphore()

    def greet(where):
        pl.semaphore_signal(barrier, inc=1, device_id=where, device_id_type=MESH)

    def greet_z(k, c):
        greet(z_peer(k))
        return c

    lax.fori_loop(1, nz, greet_z, 0)
    for k in range(1, nx):
        greet({"dp_0": x_peer(k)})
    for k in range(1, ny):
        greet({"dp_1": y_peer(k)})
    greet({"dp_2": oc})

    tbuf[h * img_dev : (h + 1) * img_dev, :] = tile[...]
    wbuf[mx, my, mc] = w_own[...]
    base = mz * tok
    here = places[...]
    found = here == base + iota((tok, img), 0)
    marks[...] = jnp.broadcast_to(jnp.sum(jnp.where(found, 1.0, 0.0), axis=1, keepdims=True), marks.shape)
    start = jnp.sum(jnp.where(here < base, 1, 0), axis=1, keepdims=True)
    slot_of = one_where(iota((SLOTS, img), 1) - start == iota((SLOTS, img), 0))
    select = dot(slot_of, one_where(found), ((1,), (1,))).astype(BF16)

    pl.semaphore_wait(barrier, (nz - 1) + (nx - 1) + (ny - 1) + 1)

    def ring(flow, step, half):
        src_block = h - (step - 1) if flow == 0 else h + (step - 1)
        dst_block = (h - step if flow == 0 else h + step) % nz
        src = tbuf.at[pl.ds(src_block * img_dev + half * half_rows, half_rows)]
        dst = tbuf.at[pl.ds(dst_block * img_dev + half * half_rows, half_rows)]
        where = {"seq": lax.rem(mz + 1, nz) if flow == 0 else lax.rem(mz + nz - 1, nz)}
        return remote(src, dst, ag_s.at[flow, step, half], ag_r.at[flow, step, half], where)

    def in_ring(flow, step, half):
        return step < h or (step == h and half == flow)

    for half in range(2):
        for flow in range(2):
            if in_ring(flow, 1, half):
                ring(flow, 1, half).start()

    def ring_step(s):
        for half in range(2):
            for flow in range(2):
                if in_ring(flow, s, half):
                    ring(flow, s, half).wait_recv()
                    if in_ring(flow, s + 1, half):
                        ring(flow, s + 1, half).start()

    def w_x(k, slot):
        return remote(wbuf.at[slot, my, mc], wbuf.at[slot, my, mc], wx_s.at[k], wx_r.at[k], {"dp_0": x_peer(k)})

    def w_y(k, slot):
        return remote(wbuf.at[:, slot, mc], wbuf.at[:, slot, mc], wy_s.at[k], wy_r.at[k], {"dp_1": y_peer(k)})

    def w_core(slot):
        return remote(wbuf.at[:, :, slot], wbuf.at[:, :, slot], wc_s, wc_r, {"dp_2": oc})

    for k in range(1, nx):
        w_x(k, mx).start()

    def send_rows(k):
        to = lax.rem(mz + k, nz)
        return remote(
            outb.at[to], inb.at[pl.ds(pl.multiple_of(mz * SLOTS, 16), SLOTS)], a2a_s.at[k], a2a_r.at[k], z_peer(k)
        )

    def take_rows(k):
        return remote(
            outb.at[0], inb.at[pl.ds(pl.multiple_of(z_source(k) * SLOTS, 16), SLOTS)], a2a_s.at[k], a2a_r.at[k], z_peer(k)
        )

    def outgoing(z):
        at = pl.ds(pl.multiple_of(z * cols, 128), cols)
        return dot(select, cot[:, at]).astype(BF16)

    def pick(k, c):
        to = lax.rem(mz + k, nz)
        outb[to] = outgoing(to)
        send_rows(k).start()
        return c

    lax.fori_loop(1, nz, pick, 0)
    inb[pl.ds(pl.multiple_of(mz * SLOTS, 16), SLOTS), :] = outgoing(mz)

    text_copy.wait()
    gacc[...] = jnp.zeros_like(gacc)

    def text_rows(i, c):
        at = pl.ds(pl.multiple_of(i * 16, 16), 16)
        squares = jnp.zeros((16, 1), F32)
        for z in range(nz):
            t = text[at, z * cols : (z + 1) * cols].astype(F32)
            squares += jnp.sum(t * t, axis=1, keepdims=True)
        inverse = jnp.where(marks[at, :1] > 0.5, 0.0, lax.rsqrt(squares / d + EPSILON))
        for z in range(nz):
            span = slice(z * cols, (z + 1) * cols)
            term = cot[at, span].astype(F32) * text[at, span].astype(F32) * inverse
            gacc[:, span] += term[:8] + term[8:]
        return c

    def text_part(first, last):
        lax.fori_loop(first, last, text_rows, 0)

    def send_gz(k):
        return remote(gz.at[lax.rem(mz + k, nz)], gz_in.at[mz], gz_s.at[k], gz_r.at[k], z_peer(k))

    def take_gz(k):
        return remote(gz.at[0], gz_in.at[z_source(k)], gz_s.at[k], gz_r.at[k], z_peer(k))

    def send_text_gain():
        for z in range(nz):
            gz[z] = jnp.sum(gacc[:, z * cols : (z + 1) * cols], axis=0, keepdims=True)

        def go(k, c):
            send_gz(k).start()
            return c

        lax.fori_loop(1, nz, go, 0)
        gz_in[mz] = gz[mz]

    def token_picks():
        slots = nz * SLOTS
        at = iota((1, slots), 1).astype(F32)
        owner = jnp.floor((at + 0.5) * (1.0 / SLOTS))
        placed = jnp.transpose(jnp.broadcast_to(here.astype(F32), (128, img)))[:, :1]
        first = jnp.sum(jnp.where(placed < owner * tok, 1.0, 0.0), axis=0, keepdims=True)
        last = jnp.sum(jnp.where(placed < owner * tok + tok, 1.0, 0.0), axis=0, keepdims=True)
        wanted = first + (at - owner * SLOTS)
        wanted = jnp.where(wanted < last, wanted, -1.0)
        for block in range(nz):
            shard = lax.rem(mz + nz - h + block, nz)
            token = (shard * img_dev + iota((img_dev, 1), 0)).astype(F32)
            picks[block * img_dev : (block + 1) * img_dev, :] = one_where(token == wanted)

    def bucket_columns():
        for at in range(0, vd, 128):
            n = min(128, vd - at)
            s = levels[:, at : at + n].astype(F32)
            r = 0.5 * row_draws[:, at : at + n]
            row = iota((128, n), 0)
            meta[at : at + n, :] = jnp.transpose(jnp.where(row == 0, s, jnp.where(row == 1, r, 0.0)))

    def pack_projector():
        wide, packed = 4 * rows, 4 * own_rows
        i, j = iota((packed, wide), 0), iota((packed, wide), 1)
        shift = jnp.zeros((packed, wide), F32)
        for b in range(4):
            hit = (j - b * rows == i - b * own_rows) & (i >= b * own_rows) & (i < (b + 1) * own_rows)
            shift = jnp.where(hit, 1.0, shift)
        shift = shift.astype(BF16)

        def pack(g, c):
            x, y = g // (ny // 2), lax.rem(g, ny // 2) * 2
            block = wbuf[x, pl.ds(y, 2)].reshape(wide, cols)
            wfull[pl.ds(pl.multiple_of(g * packed, 16), packed), :] = dot(shift, block).astype(BF16)
            return c

        lax.fori_loop(0, nx * ny // 2, pack, 0)

    token_group = GROUP * img_dev

    def token_rows(g):
        at = slice(g * token_group, (g + 1) * token_group)
        emb[at, :] = dot(tbuf[at, :], wfull[...]).astype(BF16)

    def flip(g):
        at = slice(g * token_group, (g + 1) * token_group)
        for v in range(0, vd, 640):
            n = min(640, vd - v)
            t_t[v : v + n, at] = jnp.transpose(tbuf[at, v : v + n])

    groups = nz // GROUP
    done_at = [max(abs(GROUP * g - h), abs(GROUP * g + GROUP - 1 - h)) for g in range(groups)]

    plan = {s: [] for s in range(1, h + 1)}

    def at_step(s, job):
        plan[min(max(s, 1), h)].append(job)

    def w_second():
        for k in range(1, nx):
            w_x(k, x_source(k)).wait_recv()
        for k in range(1, ny):
            w_y(k, my).start()

    def w_third():
        for k in range(1, ny):
            w_y(k, y_source(k)).wait_recv()
        w_core(mc).start()

    def w_last():
        w_core(oc).wait_recv()
        pack_projector()

    row_chunks = tok // 16
    w_done = min(5, h)
    at_step(1, lambda: text_part(0, row_chunks // 2))
    at_step(1, w_second)
    at_step(2, lambda: text_part(row_chunks // 2, row_chunks))
    at_step(2, send_text_gain)
    at_step(3, w_third)
    at_step(3, bucket_columns)
    at_step(4, token_picks)
    at_step(w_done, w_last)
    for g in sorted(range(groups), key=lambda g: done_at[g]):
        at_step(max(done_at[g], w_done), functools.partial(token_rows, g))
        at_step(done_at[g], functools.partial(flip, g))

    for s in range(1, h + 1):
        ring_step(s)
        for job in plan[s]:
            job()

    def wait_rows(k, c):
        take_rows(k).wait_recv()
        return c

    lax.fori_loop(1, nz, wait_rows, 0)
    own_gain = gain[mz]

    def token_sums(g, c):
        at = pl.ds(pl.multiple_of(g * token_group, token_group), token_group)
        e = emb[at, :].astype(F32)
        ic = dot(picks[at, :], inb[...])
        icot[at, :] = ic
        squares = jnp.sum(e * e, axis=1, keepdims=True)
        mixed = jnp.sum(ic * own_gain * e, axis=1, keepdims=True)
        lane = iota((token_group, 128), 1)
        sm_c[at, :] = jnp.where(lane == 0, squares, jnp.where(lane == 1, mixed, 0.0))
        return c

    lax.fori_loop(0, groups, token_sums, 0)
    turn = img_dev * lax.rem(mz + nz - h, nz)
    turn_back = img_dev * lax.rem(h + nz - mz, nz)
    smb[mz] = pltpu.roll(jnp.transpose(sm_c[...])[:8], turn, 1)

    def send_sums(k, source):
        return remote(smb.at[source], smb.at[source], sm_s.at[k], sm_r.at[k], z_peer(k))

    def go_sums(k, c):
        send_sums(k, mz).start()
        return c

    def wait_sums(k, c):
        send_sums(k, z_source(k)).wait_recv()
        return c

    lax.fori_loop(1, nz, go_sums, 0)
    lax.fori_loop(1, nz, wait_sums, 0)
    total = smb[0]
    for z in range(1, nz):
        total = total + smb[z]
    total = pltpu.roll(total, turn_back, 1)
    inverse = lax.rsqrt(total[0:1] / d + EPSILON)
    factor = total[1:2] * inverse / d * inverse
    row = iota((128, img), 0)
    sm_c[...] = jnp.transpose(jnp.where(row == 0, inverse, jnp.where(row == 1, factor, 0.0)))

    def token_grads(g, part):
        at = pl.ds(pl.multiple_of(g * token_group, token_group), token_group)
        e = emb[at, :].astype(F32)
        ic = icot[at, :]
        inv, fac = sm_c[at, 0:1], sm_c[at, 1:2]
        eg[at, :] = ((ic * own_gain - e * fac) * inv).astype(BF16)
        return part + jnp.sum(ic * e * inv, axis=0, keepdims=True)

    part = lax.fori_loop(0, groups, token_grads, jnp.zeros((1, cols), F32))

    def wait_gz(k, c):
        take_gz(k).wait_recv()
        return c

    lax.fori_loop(1, nz, wait_gz, 0)
    for z in range(nz):
        part = part + gz_in[z]
    g_core[mc] = part

    def gain_core(slot):
        return remote(g_core.at[slot], g_core.at[slot], gc_s, gc_r, {"dp_2": oc})

    def gain_x(k, slot):
        return remote(g_x.at[slot], g_x.at[slot], gx_s.at[k], gx_r.at[k], {"dp_0": x_peer(k)})

    def gain_y(k, slot):
        return remote(g_y.at[slot], g_y.at[slot], gy_s.at[k], gy_r.at[k], {"dp_1": y_peer(k)})

    def gain_z(k, slot):
        return remote(gain_out.at[slot], gain_out.at[slot], gf_s.at[k], gf_r.at[k], z_peer(k))

    gain_core(mc).start()

    def gain_second():
        gain_core(oc).wait_recv()
        g_x[mx] = g_core[0] + g_core[1]
        for k in range(1, nx):
            gain_x(k, mx).start()

    def gain_third():
        for k in range(1, nx):
            gain_x(k, x_source(k)).wait_recv()
        so_far = g_x[0]
        for x in range(1, nx):
            so_far = so_far + g_x[x]
        g_y[my] = so_far
        for k in range(1, ny):
            gain_y(k, my).start()

    def gain_fourth():
        for k in range(1, ny):
            gain_y(k, y_source(k)).wait_recv()
        so_far = g_y[0]
        for y in range(1, ny):
            so_far = so_far + g_y[y]
        gain_out[mz] = so_far * (1.0 / (nx * ny * 2))

        def go(k, c):
            gain_z(k, mz).start()
            return c

        lax.fori_loop(1, nz, go, 0)

    column_part = 0.5 * column_draws[...]

    def window(q):
        at = pl.ds(pl.multiple_of(2 * own_rows * q - 8 * lax.rem(q, 2), 16), win)
        grad = dot(t_t[at, :], eg[...])
        norm = jnp.sqrt(jnp.sum(grad * grad, axis=1, keepdims=True) + EPSILON)
        s, r = meta[at, 0:1], meta[at, 1:2]
        ratio = jnp.abs(grad) * (s / norm)
        lower = jnp.floor(ratio)
        quantum = lower + jnp.clip(2.0 * (ratio - lower) - (r + column_part), 0.0, 1.0)
        size = quantum * (norm / s)
        value = jnp.where(grad < 0.0, -size, size).astype(BF16)
        qq[0, q] = value[:, :hc]
        qq[1, q] = value[:, hc:]

    def swap(k, x):
        at = pl.ds(x * ny, ny)
        return remote(qq.at[oc, at], from_core.at[at], qc_s.at[k], qc_r.at[k], {"dp_2": oc})

    def send_a(k):
        return remote(s_a.at[x_peer(k)], r_a.at[mx], xa_s.at[k], xa_r.at[k], {"dp_0": x_peer(k)})

    def take_a(k):
        return remote(s_a.at[0], r_a.at[x_source(k)], xa_s.at[k], xa_r.at[k], {"dp_0": x_peer(k)})

    def send_b(k):
        return remote(s_b.at[y_peer(k)], r_b.at[my], yb_s.at[k], yb_r.at[k], {"dp_1": y_peer(k)})

    def take_b(k):
        return remote(s_b.at[0], r_b.at[y_source(k)], yb_s.at[k], yb_r.at[k], {"dp_1": y_peer(k)})

    def x_at(k):
        return lax.rem(mx + k, nx)

    def windows(k):
        x = x_at(k)

        def one(y, c):
            window(x * ny + y)
            return c

        lax.fori_loop(0, ny, one, 0)
        swap(k, x).start()

    def sum_cores(k):
        x = x_at(k)
        swap(k, x).wait_recv()

        def one(y, c):
            both = (qq[mc, x * ny + y].astype(F32) + from_core[x * ny + y].astype(F32)).astype(BF16)
            s_a[x, y] = both[:, :qc]
            s_b[y, x] = both[:, qc:]
            return c

        lax.fori_loop(0, ny, one, 0)
        if k < nx:
            send_a(k).start()

    beside = [gain_second, gain_third, gain_fourth]
    for k in range(1, nx + 1):
        windows(k)
        if beside:
            beside.pop(0)()
        if k > 1:
            sum_cores(k - 1)
    sum_cores(nx)
    for k in range(1, ny):
        send_b(k).start()
    for job in beside:
        job()

    def send_a2(k):
        return remote(t_a.at[y_peer(k)], u_a.at[my], ya_s.at[k], ya_r.at[k], {"dp_1": y_peer(k)})

    def take_a2(k):
        return remote(t_a.at[0], u_a.at[y_source(k)], ya_s.at[k], ya_r.at[k], {"dp_1": y_peer(k)})

    def send_b2(k):
        return remote(t_b.at[x_peer(k)], u_b.at[mx], xb_s.at[k], xb_r.at[k], {"dp_0": x_peer(k)})

    def take_b2(k):
        return remote(t_b.at[0], u_b.at[x_source(k)], xb_s.at[k], xb_r.at[k], {"dp_0": x_peer(k)})

    for k in range(1, nx):
        take_a(k).wait_recv()

    def add_a(y, c):
        so_far = s_a[mx, y].astype(F32)
        for k in range(1, nx):
            so_far = so_far + r_a[x_source(k), y].astype(F32)
        t_a[y] = so_far.astype(BF16)
        return c

    lax.fori_loop(0, ny, add_a, 0)
    for k in range(1, ny):
        send_a2(k).start()
    for k in range(1, ny):
        take_b(k).wait_recv()

    def add_b(x, c):
        so_far = s_b[my, x].astype(F32)
        for k in range(1, ny):
            so_far = so_far + r_b[y_source(k), x].astype(F32)
        t_b[x] = so_far.astype(BF16)
        return c

    lax.fori_loop(0, nx, add_b, 0)
    for k in range(1, nx):
        send_b2(k).start()
    share = 1.0 / (nx * ny * 2)
    for k in range(1, ny):
        take_a2(k).wait_recv()
    so_far = t_a[my].astype(F32)
    for k in range(1, ny):
        so_far = so_far + u_a[y_source(k)].astype(F32)
    fown[:, :qc] = so_far * share
    for k in range(1, nx):
        take_b2(k).wait_recv()
    so_far = t_b[mx].astype(F32)
    for k in range(1, nx):
        so_far = so_far + u_b[x_source(k)].astype(F32)
    fown[:, qc:] = so_far * share

    step = win - rows

    def rows_of(core):
        return pl.ds(pl.multiple_of(core * step, 8), rows)

    last = remote(fown.at[rows_of(oc)], f_in, f_s, f_r, {"dp_2": oc})
    last.start()
    out[:, pl.ds(pl.multiple_of(mc * hc, 128), hc)] = fown[rows_of(mc), :]
    last.wait_recv()
    out[:, pl.ds(pl.multiple_of(oc * hc, 128), hc)] = f_in[...]

    def wait_gain(k, c):
        gain_z(k, z_source(k)).wait_recv()
        gain_z(k, mz).wait_send()
        send_rows(k).wait_send()
        send_gz(k).wait_send()
        send_sums(k, mz).wait_send()
        return c

    lax.fori_loop(1, nz, wait_gain, 0)
    for s in range(1, h + 1):
        for half in range(2):
            for flow in range(2):
                if in_ring(flow, s, half):
                    ring(flow, s, half).wait_send()
    for k in range(1, nx):
        w_x(k, mx).wait_send()
        gain_x(k, mx).wait_send()
        send_a(k).wait_send()
        send_b2(k).wait_send()
    for k in range(1, ny):
        w_y(k, my).wait_send()
        gain_y(k, my).wait_send()
        send_b(k).wait_send()
        send_a2(k).wait_send()
    w_core(mc).wait_send()
    gain_core(mc).wait_send()
    for k in range(1, nx + 1):
        swap(k, x_at(k)).wait_send()
    last.wait_send()


def on_device(
    sizes, tile_tokens, proj_weight, text_hidden, cotangent, norm_gain, placeholders, bucket_levels, row_draws, column_draws
):
    nx, ny, nz = sizes
    img_dev, vd = tile_tokens.shape[1:]
    own_rows, cols = proj_weight.shape
    tok, d = text_hidden.shape[1:]
    img = placeholders.shape[1]
    rows = up(own_rows, 16)
    win = up(2 * own_rows, 16)
    windows = nx * ny
    hc, qc = cols // 2, cols // 4
    h = nz // 2
    dma = pltpu.SemaphoreType.DMA
    vmem = pl.BlockSpec(memory_space=pltpu.VMEM)
    scratch = [
        pltpu.VMEM((img, vd), BF16),
        pltpu.VMEM((vd, img), BF16),
        pltpu.VMEM((nx, ny, 2, rows, cols), BF16),
        pltpu.VMEM((vd, cols), BF16),
        pltpu.VMEM((tok, d), BF16),
        pltpu.VMEM((nz, SLOTS, cols), BF16),
        pltpu.VMEM((nz * SLOTS, cols), BF16),
        pltpu.VMEM((img, cols), BF16),
        pltpu.VMEM((img, cols), BF16),
        pltpu.VMEM((img, cols), F32),
        pltpu.VMEM((img, nz * SLOTS), BF16),
        pltpu.VMEM((img, 128), F32),
        pltpu.VMEM((nz, 8, img), F32),
        pltpu.VMEM((tok, 128), F32),
        pltpu.VMEM((8, d), F32),
        pltpu.VMEM((nz, 1, cols), F32),
        pltpu.VMEM((nz, 1, cols), F32),
        pltpu.VMEM((2, 1, cols), F32),
        pltpu.VMEM((nx, 1, cols), F32),
        pltpu.VMEM((ny, 1, cols), F32),
        pltpu.VMEM((vd, 128), F32),
        pltpu.VMEM((2, windows, win, hc), BF16),
        pltpu.VMEM((windows, win, hc), BF16),
        pltpu.VMEM((nx, ny, win, qc), BF16),
        pltpu.VMEM((ny, nx, win, qc), BF16),
        pltpu.VMEM((nx, ny, win, qc), BF16),
        pltpu.VMEM((ny, nx, win, qc), BF16),
        pltpu.VMEM((ny, win, qc), BF16),
        pltpu.VMEM((nx, win, qc), BF16),
        pltpu.VMEM((ny, win, qc), BF16),
        pltpu.VMEM((nx, win, qc), BF16),
        pltpu.VMEM((win, hc), F32),
        pltpu.VMEM((rows, hc), F32),
        dma,
        dma((2, h + 1, 2)), dma((2, h + 1, 2)),
        dma((nx,)), dma((nx,)), dma((ny,)), dma((ny,)), dma, dma,
        dma((nz,)), dma((nz,)), dma((nz,)), dma((nz,)), dma((nz,)), dma((nz,)),
        dma, dma, dma((nx,)), dma((nx,)), dma((ny,)), dma((ny,)), dma((nz,)), dma((nz,)),
        dma((nx + 1,)), dma((nx + 1,)),
        dma((nx,)), dma((nx,)), dma((ny,)), dma((ny,)), dma((ny,)), dma((ny,)), dma((nx,)), dma((nx,)), dma, dma,
    ]
    summed, gain_total = pl.pallas_call(
        functools.partial(kernel, sizes),
        out_shape=(
            jax.ShapeDtypeStruct((rows, cols), F32),
            jax.ShapeDtypeStruct((nz, 1, cols), F32),
        ),
        in_specs=[vmem] * 8 + [pl.BlockSpec(memory_space=pl.ANY)],
        out_specs=(vmem, vmem),
        scratch_shapes=scratch,
        compiler_params=pltpu.CompilerParams(
            collective_id=0, has_side_effects=True, vmem_limit_bytes=56 * 2**20
        ),
    )(
        tile_tokens[0],
        jnp.pad(proj_weight, ((0, rows - own_rows), (0, 0))),
        cotangent[0],
        norm_gain.reshape(nz, 1, cols),
        placeholders,
        bucket_levels[0],
        row_draws[0],
        column_draws,
        text_hidden[0],
    )
    odd = (lax.axis_index("dp_0") * ny + lax.axis_index("dp_1")) % 2
    core = lax.axis_index("dp_2")
    at = odd * (win - 2 * own_rows) + core * (own_rows - (win - rows))
    return lax.dynamic_slice_in_dim(summed, at, own_rows, 0), gain_total.reshape(d)


def solution(mesh):
    nz = mesh.shape["seq"]
    nx, ny = (4, 4) if mesh.shape["dp"] == 32 else (2, mesh.shape["dp"] // 4)
    finer = Mesh(mesh.devices.reshape(nx, ny, 2, nz), (*DP, "seq"))
    return jax.shard_map(
        functools.partial(on_device, (nx, ny, nz)),
        mesh=finer,
        in_specs=(
            P(DP, "seq", None),
            P(DP, "seq"),
            P(DP, "seq", None),
            P(DP, "seq", None),
            P(),
            P(DP, None),
            P(DP, "seq", None),
            P(DP, "seq", None),
            P(DP, "seq"),
        ),
        out_specs=(P(DP, "seq"), P()),
        check_vma=False,
    )
```

```python
import functools

import jax
import jax.numpy as jnp
from jax import lax
from jax.experimental import pallas as pl
from jax.experimental.pallas import tpu as pltpu
from jax.sharding import Mesh
from jax.sharding import PartitionSpec as P

DP = ("dp_0", "dp_1", "dp_2")
MESH = pl.DeviceIdType.MESH
EPSILON = 1e-06
SLOTS = 48
GROUP = 4
F32 = jnp.float32
BF16 = jnp.bfloat16


def up(n, m):
    return -(-n // m) * m


def dot(a, b, dims=((1,), (0,))):
    return lax.dot_general(a, b, (dims, ((), ())), preferred_element_type=F32)


def iota(shape, axis):
    return lax.broadcasted_iota(jnp.int32, shape, axis)


def one_where(condition):
    return jnp.where(condition, 1.0, 0.0).astype(BF16)


def kernel(
    sizes,
    tile, w_own, gain, places, levels, row_draws, column_draws, cot_hbm, text_hbm,
    out, gain_out,
    tbuf, t_t, wbuf, wfull, cot, text, outb, inb, emb, eg, icot, picks, sm_c, smb, marks, gacc,
    gz, gz_in, g_core, g_x, g_y, meta, qq, from_core, s_a, s_b, r_a, r_b, t_a, t_b, u_a, u_b, fown, f_in, grads,
    cot_sem, text_sem, ag_s, ag_r, wx_s, wx_r, wy_s, wy_r, wc_s, wc_r, a2a_s, a2a_r, sm_s, sm_r, gz_s, gz_r,
    gc_s, gc_r, gx_s, gx_r, gy_s, gy_r, gf_s, gf_r, qc_s, qc_r,
    xa_s, xa_r, ya_s, ya_r, yb_s, yb_r, xb_s, xb_r, f_s, f_r,
):
    nx, ny, nz = sizes
    own_rows, cols = w_own.shape
    rows = wbuf.shape[3]
    img_dev, vd = tile.shape
    half_rows = img_dev // 2
    img = tbuf.shape[0]
    tok, d = cot.shape
    win = qq.shape[2]
    hc = cols // 2
    qc = cols // 4
    h = nz // 2
    mx, my, mc, mz = (lax.axis_index(a) for a in ("dp_0", "dp_1", "dp_2", "seq"))
    oc = 1 - mc

    def z_peer(k):
        return {"seq": lax.rem(mz + k, nz)}

    def z_source(k):
        return lax.rem(mz + nz - k, nz)

    def x_peer(k):
        return lax.rem(mx + k, nx)

    def y_peer(k):
        return lax.rem(my + k, ny)

    def x_source(k):
        return lax.rem(mx + nx - k, nx)

    def y_source(k):
        return lax.rem(my + ny - k, ny)

    def remote(src, dst, send, recv, where):
        return pltpu.make_async_remote_copy(
            src_ref=src, dst_ref=dst, send_sem=send, recv_sem=recv, device_id=where, device_id_type=MESH
        )

    cot_copy = pltpu.make_async_copy(cot_hbm, cot, cot_sem)
    cot_copy.start()
    text_copy = pltpu.make_async_copy(text_hbm, text, text_sem)
    text_copy.start()

    barrier = pltpu.get_barrier_semaphore()

    def greet(where):
        pl.semaphore_signal(barrier, inc=1, device_id=where, device_id_type=MESH)

    def greet_z(k, c):
        greet(z_peer(k))
        return c

    lax.fori_loop(1, nz, greet_z, 0)
    for k in range(1, nx):
        greet({"dp_0": x_peer(k)})
    for k in range(1, ny):
        greet({"dp_1": y_peer(k)})
    greet({"dp_2": oc})

    tbuf[h * img_dev : (h + 1) * img_dev, :] = tile[...]
    same = iota((rows, own_rows), 0) == iota((rows, own_rows), 1)
    wbuf[mx, my, mc] = dot(one_where(same), w_own[...]).astype(BF16)
    base = mz * tok
    here = places[...]
    found = here == base + iota((tok, img), 0)
    marks[...] = jnp.broadcast_to(jnp.sum(jnp.where(found, 1.0, 0.0), axis=1, keepdims=True), marks.shape)
    start = jnp.sum(jnp.where(here < base, 1, 0), axis=1, keepdims=True)
    slot_of = one_where(iota((SLOTS, img), 1) - start == iota((SLOTS, img), 0))
    select = dot(slot_of, one_where(found), ((1,), (1,))).astype(BF16)

    pl.semaphore_wait(barrier, (nz - 1) + (nx - 1) + (ny - 1) + 1)

    def ring(flow, step, half):
        src_block = h - (step - 1) if flow == 0 else h + (step - 1)
        dst_block = (h - step if flow == 0 else h + step) % nz
        src = tbuf.at[pl.ds(src_block * img_dev + half * half_rows, half_rows)]
        dst = tbuf.at[pl.ds(dst_block * img_dev + half * half_rows, half_rows)]
        where = {"seq": lax.rem(mz + 1, nz) if flow == 0 else lax.rem(mz + nz - 1, nz)}
        return remote(src, dst, ag_s.at[flow, step, half], ag_r.at[flow, step, half], where)

    def in_ring(flow, step, half):
        return step < h or (step == h and half == flow)

    for half in range(2):
        for flow in range(2):
            if in_ring(flow, 1, half):
                ring(flow, 1, half).start()

    def ring_step(s):
        for half in range(2):
            for flow in range(2):
                if in_ring(flow, s, half):
                    ring(flow, s, half).wait_recv()
                    if in_ring(flow, s + 1, half):
                        ring(flow, s + 1, half).start()

    def w_x(k, slot):
        return remote(wbuf.at[slot, my, mc], wbuf.at[slot, my, mc], wx_s.at[k], wx_r.at[k], {"dp_0": x_peer(k)})

    def w_y(k, slot):
        return remote(wbuf.at[:, slot, mc], wbuf.at[:, slot, mc], wy_s.at[k], wy_r.at[k], {"dp_1": y_peer(k)})

    def w_core(slot):
        return remote(wbuf.at[:, :, slot], wbuf.at[:, :, slot], wc_s, wc_r, {"dp_2": oc})

    for k in range(1, nx):
        w_x(k, mx).start()

    def send_rows(k):
        to = lax.rem(mz + k, nz)
        return remote(
            outb.at[to], inb.at[pl.ds(pl.multiple_of(mz * SLOTS, 16), SLOTS)], a2a_s.at[k], a2a_r.at[k], z_peer(k)
        )

    def take_rows(k):
        return remote(
            outb.at[0], inb.at[pl.ds(pl.multiple_of(z_source(k) * SLOTS, 16), SLOTS)], a2a_s.at[k], a2a_r.at[k], z_peer(k)
        )

    def outgoing(z):
        at = pl.ds(pl.multiple_of(z * cols, 128), cols)
        return dot(select, cot[:, at]).astype(BF16)

    def pick(k, c):
        to = lax.rem(mz + k, nz)
        outb[to] = outgoing(to)
        send_rows(k).start()
        return c

    cot_copy.wait()
    lax.fori_loop(1, nz, pick, 0)
    inb[pl.ds(pl.multiple_of(mz * SLOTS, 16), SLOTS), :] = outgoing(mz)

    text_copy.wait()
    gacc[...] = jnp.zeros_like(gacc)

    def text_rows(i, c):
        at = pl.ds(pl.multiple_of(i * 16, 16), 16)
        squares = jnp.zeros((16, 1), F32)
        for z in range(nz):
            t = text[at, z * cols : (z + 1) * cols].astype(F32)
            squares += jnp.sum(t * t, axis=1, keepdims=True)
        inverse = jnp.where(marks[at, :1] > 0.5, 0.0, lax.rsqrt(squares / d + EPSILON))
        for z in range(nz):
            span = slice(z * cols, (z + 1) * cols)
            term = cot[at, span].astype(F32) * text[at, span].astype(F32) * inverse
            gacc[:, span] += term[:8] + term[8:]
        return c

    def text_part(first, last):
        lax.fori_loop(first, last, text_rows, 0)

    def send_gz(k):
        return remote(gz.at[lax.rem(mz + k, nz)], gz_in.at[mz], gz_s.at[k], gz_r.at[k], z_peer(k))

    def take_gz(k):
        return remote(gz.at[0], gz_in.at[z_source(k)], gz_s.at[k], gz_r.at[k], z_peer(k))

    def send_text_gain():
        for z in range(nz):
            gz[z] = jnp.sum(gacc[:, z * cols : (z + 1) * cols], axis=0, keepdims=True)

        def go(k, c):
            send_gz(k).start()
            return c

        lax.fori_loop(1, nz, go, 0)
        gz_in[mz] = gz[mz]

    def token_picks():
        slots = nz * SLOTS
        at = iota((1, slots), 1).astype(F32)
        owner = jnp.floor((at + 0.5) * (1.0 / SLOTS))
        placed = jnp.transpose(jnp.broadcast_to(here.astype(F32), (128, img)))[:, :1]
        first = jnp.sum(jnp.where(placed < owner * tok, 1.0, 0.0), axis=0, keepdims=True)
        last = jnp.sum(jnp.where(placed < owner * tok + tok, 1.0, 0.0), axis=0, keepdims=True)
        wanted = first + (at - owner * SLOTS)
        wanted = jnp.where(wanted < last, wanted, -1.0)
        for block in range(nz):
            shard = lax.rem(mz + nz - h + block, nz)
            token = (shard * img_dev + iota((img_dev, 1), 0)).astype(F32)
            picks[block * img_dev : (block + 1) * img_dev, :] = one_where(token == wanted)

    def bucket_columns():
        for at in range(0, vd, 128):
            n = min(128, vd - at)
            s = levels[:, at : at + n].astype(F32)
            r = 0.5 * row_draws[:, at : at + n]
            row = iota((128, n), 0)
            meta[at : at + n, :] = jnp.transpose(jnp.where(row == 0, s, jnp.where(row == 1, r, 1.0 / s)))

    def pack_projector():
        wide, packed = 4 * rows, 4 * own_rows
        i, j = iota((packed, wide), 0), iota((packed, wide), 1)
        shift = jnp.zeros((packed, wide), F32)
        for b in range(4):
            hit = (j - b * rows == i - b * own_rows) & (i >= b * own_rows) & (i < (b + 1) * own_rows)
            shift = jnp.where(hit, 1.0, shift)
        shift = shift.astype(BF16)

        def pack(g, c):
            x, y = g // (ny // 2), lax.rem(g, ny // 2) * 2
            block = wbuf[x, pl.ds(y, 2)].reshape(wide, cols)
            wfull[pl.ds(pl.multiple_of(g * packed, 16), packed), :] = dot(shift, block).astype(BF16)
            return c

        lax.fori_loop(0, nx * ny // 2, pack, 0)

    token_group = GROUP * img_dev

    def token_rows(g):
        at = slice(g * token_group, (g + 1) * token_group)
        rounded = dot(tbuf[at, :], wfull[...]).astype(BF16)
        emb[at, :] = rounded
        e = rounded.astype(F32)
        squares = jnp.sum(e * e, axis=1, keepdims=True)
        sm_c[at, :] = jnp.where(iota((token_group, 128), 1) == 0, squares, 0.0)

    def flip(g):
        at = slice(g * token_group, (g + 1) * token_group)
        for v in range(0, vd, 640):
            n = min(640, vd - v)
            t_t[v : v + n, at] = jnp.transpose(tbuf[at, v : v + n])

    groups = nz // GROUP
    done_at = [max(abs(GROUP * g - h), abs(GROUP * g + GROUP - 1 - h)) for g in range(groups)]

    plan = {s: [] for s in range(1, h + 1)}

    def at_step(s, job):
        plan[min(max(s, 1), h)].append(job)

    def w_second():
        for k in range(1, nx):
            w_x(k, x_source(k)).wait_recv()
        for k in range(1, ny):
            w_y(k, my).start()

    def w_third():
        for k in range(1, ny):
            w_y(k, y_source(k)).wait_recv()
        w_core(mc).start()

    def w_last():
        w_core(oc).wait_recv()
        pack_projector()

    row_chunks = tok // 16
    w_done = min(5, h)
    at_step(1, lambda: text_part(0, row_chunks // 2))
    at_step(1, w_second)
    at_step(2, lambda: text_part(row_chunks // 2, row_chunks))
    at_step(2, send_text_gain)
    at_step(3, w_third)
    at_step(3, bucket_columns)
    at_step(4, token_picks)
    at_step(w_done, w_last)
    for g in sorted(range(groups), key=lambda g: done_at[g]):
        at_step(max(done_at[g], w_done), functools.partial(token_rows, g))
        at_step(done_at[g], functools.partial(flip, g))

    for s in range(1, h + 1):
        ring_step(s)
        for job in plan[s]:
            job()

    def wait_rows(k, c):
        take_rows(k).wait_recv()
        return c

    lax.fori_loop(1, nz, wait_rows, 0)
    own_gain = gain[mz]

    def token_sums(g, c):
        first = pl.multiple_of(g * token_group, token_group)
        icot[pl.ds(first, token_group), :] = dot(picks[pl.ds(first, token_group), :], inb[...])
        for i in range(0, token_group, 16):
            at = pl.ds(first + i, 16)
            mixed = jnp.sum(icot[at, :] * own_gain * emb[at, :].astype(F32), axis=1, keepdims=True)
            sm_c[at, :] = jnp.where(iota((16, 128), 1) == 1, mixed, sm_c[at, :])
        return c

    lax.fori_loop(0, groups, token_sums, 0)
    turn = img_dev * lax.rem(mz + nz - h, nz)
    turn_back = img_dev * lax.rem(h + nz - mz, nz)
    smb[mz] = pltpu.roll(jnp.transpose(sm_c[...])[:8], turn, 1)[:2]

    def send_sums(k, source):
        return remote(smb.at[source], smb.at[source], sm_s.at[k], sm_r.at[k], z_peer(k))

    def go_sums(k, c):
        send_sums(k, mz).start()
        return c

    def wait_sums(k, c):
        send_sums(k, z_source(k)).wait_recv()
        return c

    lax.fori_loop(1, nz, go_sums, 0)
    lax.fori_loop(1, nz, wait_sums, 0)
    total = smb[0]
    for z in range(1, nz):
        total = total + smb[z]
    total = pltpu.roll(jnp.concatenate([total] * 4, axis=0), turn_back, 1)
    inverse = lax.rsqrt(total[0:1] / d + EPSILON)
    factor = total[1:2] * inverse / d * inverse
    row = iota((128, img), 0)
    sm_c[...] = jnp.transpose(jnp.where(row == 0, inverse, jnp.where(row == 1, factor, 0.0)))

    def token_grads(g, part):
        first = pl.multiple_of(g * token_group, token_group)
        for i in range(0, token_group, 16):
            at = pl.ds(first + i, 16)
            e = emb[at, :].astype(F32)
            ic = icot[at, :]
            inv, fac = sm_c[at, 0:1], sm_c[at, 1:2]
            eg[at, :] = ((ic * own_gain - e * fac) * inv).astype(BF16)
            term = ic * e * inv
            part = part + term[:8] + term[8:]
        return part

    part = lax.fori_loop(0, groups, token_grads, jnp.zeros((8, cols), F32))
    part = jnp.sum(part, axis=0, keepdims=True)

    def wait_gz(k, c):
        take_gz(k).wait_recv()
        return c

    lax.fori_loop(1, nz, wait_gz, 0)
    for z in range(nz):
        part = part + gz_in[z]
    g_core[mc] = part

    def gain_core(slot):
        return remote(g_core.at[slot], g_core.at[slot], gc_s, gc_r, {"dp_2": oc})

    def gain_x(k, slot):
        return remote(g_x.at[slot], g_x.at[slot], gx_s.at[k], gx_r.at[k], {"dp_0": x_peer(k)})

    def gain_y(k, slot):
        return remote(g_y.at[slot], g_y.at[slot], gy_s.at[k], gy_r.at[k], {"dp_1": y_peer(k)})

    def gain_z(k, slot):
        return remote(gain_out.at[slot], gain_out.at[slot], gf_s.at[k], gf_r.at[k], z_peer(k))

    gain_core(mc).start()

    def gain_second():
        gain_core(oc).wait_recv()
        g_x[mx] = g_core[0] + g_core[1]
        for k in range(1, nx):
            gain_x(k, mx).start()

    def gain_third():
        for k in range(1, nx):
            gain_x(k, x_source(k)).wait_recv()
        so_far = g_x[0]
        for x in range(1, nx):
            so_far = so_far + g_x[x]
        g_y[my] = so_far
        for k in range(1, ny):
            gain_y(k, my).start()

    def gain_fourth():
        for k in range(1, ny):
            gain_y(k, y_source(k)).wait_recv()
        so_far = g_y[0]
        for y in range(1, ny):
            so_far = so_far + g_y[y]
        gain_out[mz] = so_far * (1.0 / (nx * ny * 2))

        def go(k, c):
            gain_z(k, mz).start()
            return c

        lax.fori_loop(1, nz, go, 0)

    column_part = 0.5 * column_draws[...]

    def first_row(q):
        return pl.multiple_of(2 * own_rows * q - 8 * lax.rem(q, 2), 8)

    def window(q, slot):
        grads[slot] = dot(t_t[pl.ds(pl.multiple_of(first_row(q), 16), win), :], eg[...])

    def quantize(q, slot):
        for i in range(0, win, 16):
            grad = grads[slot, i : i + 16, :]
            at = pl.ds(first_row(q) + i, 16)
            square = jnp.sum(grad * grad, axis=1, keepdims=True) + EPSILON
            root = lax.rsqrt(square)
            s, r, s_inverse = meta[at, 0:1], meta[at, 1:2], meta[at, 2:3]
            ratio = jnp.abs(grad) * (s * root)
            lower = jnp.floor(ratio)
            quantum = lower + jnp.clip(2.0 * (ratio - lower) - (r + column_part), 0.0, 1.0)
            size = quantum * (square * root * s_inverse)
            value = jnp.where(grad < 0.0, -size, size).astype(BF16)
            qq[0, q, i : i + 16, :] = value[:, :hc]
            qq[1, q, i : i + 16, :] = value[:, hc:]

    def swap(k, x):
        at = pl.ds(x * ny, ny)
        return remote(qq.at[oc, at], from_core.at[at], qc_s.at[k], qc_r.at[k], {"dp_2": oc})

    def send_a(k):
        return remote(s_a.at[x_peer(k)], r_a.at[mx], xa_s.at[k], xa_r.at[k], {"dp_0": x_peer(k)})

    def take_a(k):
        return remote(s_a.at[0], r_a.at[x_source(k)], xa_s.at[k], xa_r.at[k], {"dp_0": x_peer(k)})

    def send_b(k, j):
        x = x_at(k)
        return remote(s_b.at[y_peer(j), x], r_b.at[my, x], yb_s.at[k, j], yb_r.at[k, j], {"dp_1": y_peer(j)})

    def take_b(k, j):
        x = x_at(k)
        return remote(s_b.at[0, x], r_b.at[y_source(j), x], yb_s.at[k, j], yb_r.at[k, j], {"dp_1": y_peer(j)})

    def x_at(k):
        return lax.rem(mx + k, nx)

    def windows(k):
        x = x_at(k)

        def two(pair, c):
            q = x * ny + 2 * pair
            window(q, 0)
            window(q + 1, 1)
            quantize(q, 0)
            quantize(q + 1, 1)
            return c

        lax.fori_loop(0, ny // 2, two, 0)
        swap(k, x).start()

    def sum_cores(k):
        x = x_at(k)
        swap(k, x).wait_recv()

        def one(y, c):
            both = (qq[mc, x * ny + y].astype(F32) + from_core[x * ny + y].astype(F32)).astype(BF16)
            s_a[x, y] = both[:, :qc]
            s_b[y, x] = both[:, qc:]
            return c

        lax.fori_loop(0, ny, one, 0)
        if k < nx:
            send_a(k).start()
        for j in range(1, ny):
            send_b(k, j).start()

    def send_a2(k):
        return remote(t_a.at[y_peer(k)], u_a.at[my], ya_s.at[k], ya_r.at[k], {"dp_1": y_peer(k)})

    def take_a2(k):
        return remote(t_a.at[0], u_a.at[y_source(k)], ya_s.at[k], ya_r.at[k], {"dp_1": y_peer(k)})

    def send_b2(k):
        return remote(t_b.at[x_peer(k)], u_b.at[mx], xb_s.at[k], xb_r.at[k], {"dp_0": x_peer(k)})

    def take_b2(k):
        return remote(t_b.at[0], u_b.at[x_source(k)], xb_s.at[k], xb_r.at[k], {"dp_0": x_peer(k)})

    def sum_b(k):
        x = x_at(k)
        for j in range(1, ny):
            take_b(k, j).wait_recv()
        so_far = s_b[my, x].astype(F32)
        for j in range(1, ny):
            so_far = so_far + r_b[y_source(j), x].astype(F32)
        t_b[x] = so_far.astype(BF16)
        if k < nx:
            send_b2(k).start()

    def add_a(y, c):
        so_far = s_a[mx, y].astype(F32)
        for k in range(1, nx):
            so_far = so_far + r_a[x_source(k), y].astype(F32)
        t_a[y] = so_far.astype(BF16)
        return c

    def sum_a():
        for k in range(1, nx):
            take_a(k).wait_recv()
        lax.fori_loop(0, ny, add_a, 0)
        for k in range(1, ny):
            send_a2(k).start()

    beside = [gain_second, gain_third, gain_fourth]
    for k in range(1, nx + 1):
        windows(k)
        if beside:
            beside.pop(0)()
        if k > 1:
            sum_cores(k - 1)
        if k > 2:
            sum_b(k - 2)
    sum_cores(nx)
    for job in beside:
        job()
    sum_b(nx - 1)
    sum_a()
    sum_b(nx)
    share = 1.0 / (nx * ny * 2)
    for k in range(1, ny):
        take_a2(k).wait_recv()
    so_far = t_a[my].astype(F32)
    for k in range(1, ny):
        so_far = so_far + u_a[y_source(k)].astype(F32)
    fown[:, :qc] = so_far * share
    for k in range(1, nx):
        take_b2(k).wait_recv()
    so_far = t_b[mx].astype(F32)
    for k in range(1, nx):
        so_far = so_far + u_b[x_source(k)].astype(F32)
    fown[:, qc:] = so_far * share

    step = win - rows

    def rows_of(core):
        return pl.ds(pl.multiple_of(core * step, 8), rows)

    last = remote(fown.at[rows_of(oc)], f_in, f_s, f_r, {"dp_2": oc})
    last.start()
    out[:, pl.ds(pl.multiple_of(mc * hc, 128), hc)] = fown[rows_of(mc), :]
    last.wait_recv()
    out[:, pl.ds(pl.multiple_of(oc * hc, 128), hc)] = f_in[...]

    def wait_gain(k, c):
        gain_z(k, z_source(k)).wait_recv()
        gain_z(k, mz).wait_send()
        send_rows(k).wait_send()
        send_gz(k).wait_send()
        send_sums(k, mz).wait_send()
        return c

    lax.fori_loop(1, nz, wait_gain, 0)
    for s in range(1, h + 1):
        for half in range(2):
            for flow in range(2):
                if in_ring(flow, s, half):
                    ring(flow, s, half).wait_send()
    for k in range(1, nx):
        w_x(k, mx).wait_send()
        gain_x(k, mx).wait_send()
        send_a(k).wait_send()
        send_b2(k).wait_send()
    for k in range(1, ny):
        w_y(k, my).wait_send()
        gain_y(k, my).wait_send()
        send_a2(k).wait_send()
    w_core(mc).wait_send()
    gain_core(mc).wait_send()
    for k in range(1, nx + 1):
        swap(k, x_at(k)).wait_send()
        for j in range(1, ny):
            send_b(k, j).wait_send()
    last.wait_send()


def finish(ny, for_odd, for_core, summed, gain, weight_out, gain_out):
    odd = lax.rem(lax.axis_index("dp_1"), 2)
    at = odd * for_odd + lax.axis_index("dp_2") * for_core
    rows = summed.shape[0]
    weight_out[...] = pltpu.roll(summed[...], lax.rem(rows - at, rows), 0)[: weight_out.shape[0]]
    gain_out[...] = gain[...]


def on_device(
    sizes, tile_tokens, proj_weight, text_hidden, cotangent, norm_gain, placeholders, bucket_levels, row_draws, column_draws
):
    nx, ny, nz = sizes
    img_dev, vd = tile_tokens.shape[1:]
    own_rows, cols = proj_weight.shape
    tok, d = text_hidden.shape[1:]
    img = placeholders.shape[1]
    rows = up(own_rows, 16)
    win = up(2 * own_rows, 16)
    windows = nx * ny
    hc, qc = cols // 2, cols // 4
    h = nz // 2
    dma = pltpu.SemaphoreType.DMA
    vmem = pl.BlockSpec(memory_space=pltpu.VMEM)
    scratch = [
        pltpu.VMEM((img, vd), BF16),
        pltpu.VMEM((vd, img), BF16),
        pltpu.VMEM((nx, ny, 2, rows, cols), BF16),
        pltpu.VMEM((vd, cols), BF16),
        pltpu.VMEM((tok, d), BF16),
        pltpu.VMEM((tok, d), BF16),
        pltpu.VMEM((nz, SLOTS, cols), BF16),
        pltpu.VMEM((nz * SLOTS, cols), BF16),
        pltpu.VMEM((img, cols), BF16),
        pltpu.VMEM((img, cols), BF16),
        pltpu.VMEM((img, cols), F32),
        pltpu.VMEM((img, nz * SLOTS), BF16),
        pltpu.VMEM((img, 128), F32),
        pltpu.VMEM((nz, 2, img), F32),
        pltpu.VMEM((tok, 128), F32),
        pltpu.VMEM((8, d), F32),
        pltpu.VMEM((nz, 1, cols), F32),
        pltpu.VMEM((nz, 1, cols), F32),
        pltpu.VMEM((2, 1, cols), F32),
        pltpu.VMEM((nx, 1, cols), F32),
        pltpu.VMEM((ny, 1, cols), F32),
        pltpu.VMEM((vd, 128), F32),
        pltpu.VMEM((2, windows, win, hc), BF16),
        pltpu.VMEM((windows, win, hc), BF16),
        pltpu.VMEM((nx, ny, win, qc), BF16),
        pltpu.VMEM((ny, nx, win, qc), BF16),
        pltpu.VMEM((nx, ny, win, qc), BF16),
        pltpu.VMEM((ny, nx, win, qc), BF16),
        pltpu.VMEM((ny, win, qc), BF16),
        pltpu.VMEM((nx, win, qc), BF16),
        pltpu.VMEM((ny, win, qc), BF16),
        pltpu.VMEM((nx, win, qc), BF16),
        pltpu.VMEM((win, hc), F32),
        pltpu.VMEM((rows, hc), F32),
        pltpu.VMEM((2, win, cols), F32),
        dma, dma,
        dma((2, h + 1, 2)), dma((2, h + 1, 2)),
        dma((nx,)), dma((nx,)), dma((ny,)), dma((ny,)), dma, dma,
        dma((nz,)), dma((nz,)), dma((nz,)), dma((nz,)), dma((nz,)), dma((nz,)),
        dma, dma, dma((nx,)), dma((nx,)), dma((ny,)), dma((ny,)), dma((nz,)), dma((nz,)),
        dma((nx + 1,)), dma((nx + 1,)),
        dma((nx,)), dma((nx,)), dma((ny,)), dma((ny,)), dma((nx + 1, ny)), dma((nx + 1, ny)), dma((nx,)), dma((nx,)), dma, dma,
    ]
    summed, gain_total = pl.pallas_call(
        functools.partial(kernel, sizes),
        out_shape=(
            jax.ShapeDtypeStruct((rows, cols), F32),
            jax.ShapeDtypeStruct((nz, 1, cols), F32),
        ),
        in_specs=[vmem] * 7 + [pl.BlockSpec(memory_space=pl.ANY)] * 2,
        out_specs=(vmem, vmem),
        scratch_shapes=scratch,
        compiler_params=pltpu.CompilerParams(
            collective_id=0, has_side_effects=True, vmem_limit_bytes=58 * 2**20
        ),
    )(
        tile_tokens[0],
        proj_weight,
        norm_gain.reshape(nz, 1, cols),
        placeholders,
        bucket_levels[0],
        row_draws[0],
        column_draws,
        cotangent[0],
        text_hidden[0],
    )
    weight, gain_grad = pl.pallas_call(
        functools.partial(finish, ny, win - 2 * own_rows, own_rows - (win - rows)),
        out_shape=(
            jax.ShapeDtypeStruct((own_rows, cols), F32),
            jax.ShapeDtypeStruct((nz, 1, cols), F32),
        ),
        in_specs=[vmem, vmem],
        out_specs=(vmem, vmem),
    )(summed, gain_total)
    return weight, gain_grad.reshape(d)


def solution(mesh):
    nz = mesh.shape["seq"]
    nx, ny = (4, 4) if mesh.shape["dp"] == 32 else (2, mesh.shape["dp"] // 4)
    finer = Mesh(mesh.devices.reshape(nx, ny, 2, nz), (*DP, "seq"))
    return jax.shard_map(
        functools.partial(on_device, (nx, ny, nz)),
        mesh=finer,
        in_specs=(
            P(DP, "seq", None),
            P(DP, "seq"),
            P(DP, "seq", None),
            P(DP, "seq", None),
            P(),
            P(DP, None),
            P(DP, "seq", None),
            P(DP, "seq", None),
            P(DP, "seq"),
        ),
        out_specs=(P(DP, "seq"), P()),
        check_vma=False,
    )
```

```python
import functools

import jax
import jax.numpy as jnp
from jax import lax
from jax.experimental import pallas as pl
from jax.experimental.pallas import tpu as pltpu
from jax.sharding import Mesh
from jax.sharding import PartitionSpec as P

DP = ("dp_0", "dp_1", "dp_2")
MESH = pl.DeviceIdType.MESH
EPSILON = 1e-06
SLOTS = 48
GROUP = 4
ORDER = (8, 1, 15, 7, 9, 2, 14, 6, 10, 3, 13, 5, 11, 4, 12)
ROWS_AT_STEP = (3, 2, 2, 2, 2, 2, 2, 0, 0)
F32 = jnp.float32
BF16 = jnp.bfloat16


def up(n, m):
    return -(-n // m) * m


def dot(a, b, dims=((1,), (0,))):
    return lax.dot_general(a, b, (dims, ((), ())), preferred_element_type=F32)


def iota(shape, axis):
    return lax.broadcasted_iota(jnp.int32, shape, axis)


def one_where(condition):
    return jnp.where(condition, 1.0, 0.0).astype(BF16)


def kernel(
    sizes,
    tile, w_own, gain, places, levels, row_draws, column_draws, cot_hbm, text_hbm,
    out, gain_out,
    tbuf, t_t, wbuf, wfull, cot, text, outb, inb, emb, eg, icot, picks, sm_c, smb, marks, gacc,
    gz, gz_in, g_core, g_x, g_y, meta, qq, from_core, s_a, s_b, r_a, r_b, t_a, t_b, u_a, u_b, grads,
    cot_sem, text_sem, ag_s, ag_r, wx_s, wx_r, wy_s, wy_r, wc_s, wc_r, a2a_s, a2a_r, sm_s, sm_r, gz_s, gz_r,
    gc_s, gc_r, gx_s, gx_r, gy_s, gy_r, gf_s, gf_r, qc_s, qc_r,
    xa_s, xa_r, ya_s, ya_r, yb_s, yb_r, xb_s, xb_r,
):
    nx, ny, nz = sizes
    own_rows, cols = w_own.shape
    rows = wbuf.shape[3]
    img_dev, vd = tile.shape
    half_rows = img_dev // 2
    img = tbuf.shape[0]
    tok, d = cot.shape
    win = qq.shape[1]
    hc = cols // 2
    h = nz // 2
    mx, my, mc, mz = (lax.axis_index(a) for a in ("dp_0", "dp_1", "dp_2", "seq"))
    oc = 1 - mc

    def z_peer(k):
        return {"seq": lax.rem(mz + k, nz)}

    def z_source(k):
        return lax.rem(mz + nz - k, nz)

    def x_peer(k):
        return lax.rem(mx + k, nx)

    def y_peer(k):
        return lax.rem(my + k, ny)

    def x_source(k):
        return lax.rem(mx + nx - k, nx)

    def y_source(k):
        return lax.rem(my + ny - k, ny)

    def remote(src, dst, send, recv, where):
        return pltpu.make_async_remote_copy(
            src_ref=src, dst_ref=dst, send_sem=send, recv_sem=recv, device_id=where, device_id_type=MESH
        )

    cot_copy = pltpu.make_async_copy(cot_hbm, cot, cot_sem)
    cot_copy.start()
    text_copy = pltpu.make_async_copy(text_hbm, text, text_sem)
    text_copy.start()

    barrier = pltpu.get_barrier_semaphore()

    def greet(where):
        pl.semaphore_signal(barrier, inc=1, device_id=where, device_id_type=MESH)

    def greet_z(k, c):
        greet(z_peer(k))
        return c

    lax.fori_loop(1, nz, greet_z, 0)
    for k in range(1, nx):
        greet({"dp_0": x_peer(k)})
    for k in range(1, ny):
        greet({"dp_1": y_peer(k)})
    greet({"dp_2": oc})

    tbuf[h * img_dev : (h + 1) * img_dev, :] = tile[...]
    same = iota((rows, own_rows), 0) == iota((rows, own_rows), 1)
    wbuf[mx, my, mc] = dot(one_where(same), w_own[...]).astype(BF16)
    base = mz * tok
    here = places[...]
    found = here == base + iota((tok, img), 0)
    marks[...] = jnp.broadcast_to(jnp.sum(jnp.where(found, 1.0, 0.0), axis=1, keepdims=True), marks.shape)
    start = jnp.sum(jnp.where(here < base, 1, 0), axis=1, keepdims=True)
    slot_of = one_where(iota((SLOTS, img), 1) - start == iota((SLOTS, img), 0))
    select = dot(slot_of, one_where(found), ((1,), (1,))).astype(BF16)

    pl.semaphore_wait(barrier, (nz - 1) + (nx - 1) + (ny - 1) + 1)

    def ring(flow, step, half):
        src_block = h - (step - 1) if flow == 0 else h + (step - 1)
        dst_block = (h - step if flow == 0 else h + step) % nz
        src = tbuf.at[pl.ds(src_block * img_dev + half * half_rows, half_rows)]
        dst = tbuf.at[pl.ds(dst_block * img_dev + half * half_rows, half_rows)]
        where = {"seq": lax.rem(mz + 1, nz) if flow == 0 else lax.rem(mz + nz - 1, nz)}
        return remote(src, dst, ag_s.at[flow, step, half], ag_r.at[flow, step, half], where)

    def in_ring(flow, step, half):
        return step < h or (step == h and half == flow)

    for half in range(2):
        for flow in range(2):
            if in_ring(flow, 1, half):
                ring(flow, 1, half).start()

    def ring_step(s):
        for half in range(2):
            for flow in range(2):
                if in_ring(flow, s, half):
                    ring(flow, s, half).wait_recv()
                    if in_ring(flow, s + 1, half):
                        ring(flow, s + 1, half).start()

    def w_x(k, slot):
        return remote(wbuf.at[slot, my, mc], wbuf.at[slot, my, mc], wx_s.at[k], wx_r.at[k], {"dp_0": x_peer(k)})

    def w_y(k, slot):
        return remote(wbuf.at[:, slot, mc], wbuf.at[:, slot, mc], wy_s.at[k], wy_r.at[k], {"dp_1": y_peer(k)})

    def w_core(slot):
        return remote(wbuf.at[:, :, slot], wbuf.at[:, :, slot], wc_s, wc_r, {"dp_2": oc})

    for k in range(1, nx):
        w_x(k, mx).start()

    def send_rows(k):
        to = lax.rem(mz + k, nz)
        return remote(
            outb.at[to], inb.at[pl.ds(pl.multiple_of(mz * SLOTS, 16), SLOTS)], a2a_s.at[k], a2a_r.at[k], z_peer(k)
        )

    def take_rows(k):
        return remote(
            outb.at[0], inb.at[pl.ds(pl.multiple_of(z_source(k) * SLOTS, 16), SLOTS)], a2a_s.at[k], a2a_r.at[k], z_peer(k)
        )

    def outgoing(z):
        at = pl.ds(pl.multiple_of(z * cols, 128), cols)
        return dot(select, cot[:, at]).astype(BF16)

    def pick(k):
        to = lax.rem(mz + k, nz)
        outb[to] = outgoing(to)
        send_rows(k).start()

    order = list(ORDER) if nz == 16 else list(range(1, nz))

    def pick_some(step):
        amount = ROWS_AT_STEP[step] if nz == 16 else nz
        for k in order[:amount]:
            pick(k)
        del order[:amount]

    cot_copy.wait()
    pick_some(0)
    inb[pl.ds(pl.multiple_of(mz * SLOTS, 16), SLOTS), :] = outgoing(mz)

    text_copy.wait()
    gacc[...] = jnp.zeros_like(gacc)

    def text_rows(i, c):
        at = pl.ds(pl.multiple_of(i * 16, 16), 16)
        squares = jnp.zeros((16, 1), F32)
        for z in range(nz):
            t = text[at, z * cols : (z + 1) * cols].astype(F32)
            squares += jnp.sum(t * t, axis=1, keepdims=True)
        inverse = jnp.where(marks[at, :1] > 0.5, 0.0, lax.rsqrt(squares / d + EPSILON))
        for z in range(nz):
            span = slice(z * cols, (z + 1) * cols)
            term = cot[at, span].astype(F32) * text[at, span].astype(F32) * inverse
            gacc[:, span] += term[:8] + term[8:]
        return c

    def text_part(first, last):
        lax.fori_loop(first, last, text_rows, 0)

    def send_gz(k):
        return remote(gz.at[lax.rem(mz + k, nz)], gz_in.at[mz], gz_s.at[k], gz_r.at[k], z_peer(k))

    def take_gz(k):
        return remote(gz.at[0], gz_in.at[z_source(k)], gz_s.at[k], gz_r.at[k], z_peer(k))

    def send_text_gain():
        for z in range(nz):
            gz[z] = jnp.sum(gacc[:, z * cols : (z + 1) * cols], axis=0, keepdims=True)

        def go(k, c):
            send_gz(k).start()
            return c

        lax.fori_loop(1, nz, go, 0)
        gz_in[mz] = gz[mz]

    def token_picks():
        slots = nz * SLOTS
        at = iota((1, slots), 1).astype(F32)
        owner = jnp.floor((at + 0.5) * (1.0 / SLOTS))
        placed = jnp.transpose(jnp.broadcast_to(here.astype(F32), (128, img)))[:, :1]
        first = jnp.sum(jnp.where(placed < owner * tok, 1.0, 0.0), axis=0, keepdims=True)
        last = jnp.sum(jnp.where(placed < owner * tok + tok, 1.0, 0.0), axis=0, keepdims=True)
        wanted = first + (at - owner * SLOTS)
        wanted = jnp.where(wanted < last, wanted, -1.0)
        for block in range(nz):
            shard = lax.rem(mz + nz - h + block, nz)
            token = (shard * img_dev + iota((img_dev, 1), 0)).astype(F32)
            picks[block * img_dev : (block + 1) * img_dev, :] = one_where(token == wanted)

    def bucket_columns():
        for at in range(0, vd, 128):
            n = min(128, vd - at)
            s = levels[:, at : at + n].astype(F32)
            r = 0.5 * row_draws[:, at : at + n]
            row = iota((128, n), 0)
            meta[at : at + n, :] = jnp.transpose(jnp.where(row == 0, s, jnp.where(row == 1, r, 1.0 / s)))

    def pack_projector():
        wide, packed = 4 * rows, 4 * own_rows
        i, j = iota((packed, wide), 0), iota((packed, wide), 1)
        shift = jnp.zeros((packed, wide), F32)
        for b in range(4):
            hit = (j - b * rows == i - b * own_rows) & (i >= b * own_rows) & (i < (b + 1) * own_rows)
            shift = jnp.where(hit, 1.0, shift)
        shift = shift.astype(BF16)

        def pack(g, c):
            x, y = g // (ny // 2), lax.rem(g, ny // 2) * 2
            block = wbuf[x, pl.ds(y, 2)].reshape(wide, cols)
            wfull[pl.ds(pl.multiple_of(g * packed, 16), packed), :] = dot(shift, block).astype(BF16)
            return c

        lax.fori_loop(0, nx * ny // 2, pack, 0)

    token_group = GROUP * img_dev

    def token_rows(g):
        at = slice(g * token_group, (g + 1) * token_group)
        rounded = dot(tbuf[at, :], wfull[...]).astype(BF16)
        emb[at, :] = rounded
        e = rounded.astype(F32)
        squares = jnp.sum(e * e, axis=1, keepdims=True)
        sm_c[at, :] = jnp.where(iota((token_group, 128), 1) == 0, squares, 0.0)

    def flip(g):
        at = slice(g * token_group, (g + 1) * token_group)
        for v in range(0, vd, 640):
            n = min(640, vd - v)
            t_t[v : v + n, at] = jnp.transpose(tbuf[at, v : v + n])

    groups = nz // GROUP
    done_at = [max(abs(GROUP * g - h), abs(GROUP * g + GROUP - 1 - h)) for g in range(groups)]

    plan = {s: [] for s in range(1, h + 1)}

    def at_step(s, job):
        plan[min(max(s, 1), h)].append(job)

    def w_second():
        for k in range(1, nx):
            w_x(k, x_source(k)).wait_recv()
        for k in range(1, ny):
            w_y(k, my).start()

    def w_third():
        for k in range(1, ny):
            w_y(k, y_source(k)).wait_recv()
        w_core(mc).start()

    def w_last():
        w_core(oc).wait_recv()
        pack_projector()

    row_chunks = tok // 16
    w_done = min(5, h)
    at_step(1, lambda: text_part(0, row_chunks // 2))
    at_step(1, w_second)
    at_step(2, lambda: text_part(row_chunks // 2, row_chunks))
    at_step(2, send_text_gain)
    at_step(3, w_third)
    at_step(3, bucket_columns)
    at_step(4, token_picks)
    at_step(w_done, w_last)
    for g in sorted(range(groups), key=lambda g: done_at[g]):
        at_step(max(done_at[g], w_done), functools.partial(token_rows, g))
        at_step(done_at[g], functools.partial(flip, g))

    for s in range(1, h + 1):
        ring_step(s)
        if order:
            pick_some(s)
        for job in plan[s]:
            job()

    def wait_rows(k, c):
        take_rows(k).wait_recv()
        return c

    lax.fori_loop(1, nz, wait_rows, 0)
    own_gain = gain[mz]

    def token_sums(g, c):
        first = pl.multiple_of(g * token_group, token_group)
        icot[pl.ds(first, token_group), :] = dot(picks[pl.ds(first, token_group), :], inb[...])
        for i in range(0, token_group, 16):
            at = pl.ds(first + i, 16)
            mixed = jnp.sum(icot[at, :] * own_gain * emb[at, :].astype(F32), axis=1, keepdims=True)
            sm_c[at, :] = jnp.where(iota((16, 128), 1) == 1, mixed, sm_c[at, :])
        return c

    lax.fori_loop(0, groups, token_sums, 0)
    turn = img_dev * lax.rem(mz + nz - h, nz)
    turn_back = img_dev * lax.rem(h + nz - mz, nz)
    smb[mz] = pltpu.roll(jnp.transpose(sm_c[...])[:8], turn, 1)[:2]

    def send_sums(k, source):
        return remote(smb.at[source], smb.at[source], sm_s.at[k], sm_r.at[k], z_peer(k))

    def go_sums(k, c):
        send_sums(k, mz).start()
        return c

    def wait_sums(k, c):
        send_sums(k, z_source(k)).wait_recv()
        return c

    lax.fori_loop(1, nz, go_sums, 0)
    lax.fori_loop(1, nz, wait_sums, 0)
    total = smb[0]
    for z in range(1, nz):
        total = total + smb[z]
    total = pltpu.roll(jnp.concatenate([total] * 4, axis=0), turn_back, 1)
    inverse = lax.rsqrt(total[0:1] / d + EPSILON)
    factor = total[1:2] * inverse / d * inverse
    row = iota((128, img), 0)
    sm_c[...] = jnp.transpose(jnp.where(row == 0, inverse, jnp.where(row == 1, factor, 0.0)))

    def token_grads(g, part):
        first = pl.multiple_of(g * token_group, token_group)
        for i in range(0, token_group, 16):
            at = pl.ds(first + i, 16)
            e = emb[at, :].astype(F32)
            ic = icot[at, :]
            inv, fac = sm_c[at, 0:1], sm_c[at, 1:2]
            eg[at, :] = ((ic * own_gain - e * fac) * inv).astype(BF16)
            term = ic * e * inv
            part = part + term[:8] + term[8:]
        return part

    part = lax.fori_loop(0, groups, token_grads, jnp.zeros((8, cols), F32))
    part = jnp.sum(part, axis=0, keepdims=True)

    def wait_gz(k, c):
        take_gz(k).wait_recv()
        return c

    lax.fori_loop(1, nz, wait_gz, 0)
    for z in range(nz):
        part = part + gz_in[z]
    g_core[mc] = part

    def gain_core(slot):
        return remote(g_core.at[slot], g_core.at[slot], gc_s, gc_r, {"dp_2": oc})

    def gain_x(k, slot):
        return remote(g_x.at[slot], g_x.at[slot], gx_s.at[k], gx_r.at[k], {"dp_0": x_peer(k)})

    def gain_y(k, slot):
        return remote(g_y.at[slot], g_y.at[slot], gy_s.at[k], gy_r.at[k], {"dp_1": y_peer(k)})

    def gain_z(k, slot):
        return remote(gain_out.at[slot], gain_out.at[slot], gf_s.at[k], gf_r.at[k], z_peer(k))

    gain_core(mc).start()

    def gain_second():
        gain_core(oc).wait_recv()
        g_x[mx] = g_core[0] + g_core[1]
        for k in range(1, nx):
            gain_x(k, mx).start()

    def gain_third():
        for k in range(1, nx):
            gain_x(k, x_source(k)).wait_recv()
        so_far = g_x[0]
        for x in range(1, nx):
            so_far = so_far + g_x[x]
        g_y[my] = so_far
        for k in range(1, ny):
            gain_y(k, my).start()

    def gain_fourth():
        for k in range(1, ny):
            gain_y(k, y_source(k)).wait_recv()
        so_far = g_y[0]
        for y in range(1, ny):
            so_far = so_far + g_y[y]
        gain_out[mz] = so_far * (1.0 / (nx * ny * 2))

        def go(k, c):
            gain_z(k, mz).start()
            return c

        lax.fori_loop(1, nz, go, 0)

    column_part = 0.5 * column_draws[...]

    def first_row(q):
        return pl.multiple_of(2 * own_rows * q - 8 * lax.rem(q, 2), 8)

    def window(q, slot):
        grads[slot] = dot(t_t[pl.ds(pl.multiple_of(first_row(q), 16), win), :], eg[...])

    def quantize(q, slot):
        for i in range(0, win, 16):
            grad = grads[slot, i : i + 16, :]
            at = pl.ds(first_row(q) + i, 16)
            square = jnp.sum(grad * grad, axis=1, keepdims=True) + EPSILON
            root = lax.rsqrt(square)
            s, r, s_inverse = meta[at, 0:1], meta[at, 1:2], meta[at, 2:3]
            ratio = jnp.abs(grad) * (s * root)
            lower = jnp.floor(ratio)
            quantum = lower + jnp.clip(2.0 * (ratio - lower) - (r + column_part), 0.0, 1.0)
            size = quantum * (square * root * s_inverse)
            value = jnp.where(grad < 0.0, -size, size).astype(BF16)
            qq[q, i : i + 16, :] = value

    def rows_of(core):
        return pl.ds(pl.multiple_of(core * (win - rows), 16), rows)

    def swap(k, x):
        at = pl.ds(x * ny, ny)
        return remote(qq.at[at, rows_of(oc)], from_core.at[at], qc_s.at[k], qc_r.at[k], {"dp_2": oc})

    def send_a(k):
        return remote(s_a.at[x_peer(k)], r_a.at[mx], xa_s.at[k], xa_r.at[k], {"dp_0": x_peer(k)})

    def take_a(k):
        return remote(s_a.at[0], r_a.at[x_source(k)], xa_s.at[k], xa_r.at[k], {"dp_0": x_peer(k)})

    def send_b(k, j):
        x = x_at(k)
        return remote(s_b.at[y_peer(j), x], r_b.at[my, x], yb_s.at[k, j], yb_r.at[k, j], {"dp_1": y_peer(j)})

    def take_b(k, j):
        x = x_at(k)
        return remote(s_b.at[0, x], r_b.at[y_source(j), x], yb_s.at[k, j], yb_r.at[k, j], {"dp_1": y_peer(j)})

    def x_at(k):
        return lax.rem(mx + k, nx)

    def windows(k):
        x = x_at(k)

        def two(pair, c):
            q = x * ny + 2 * pair
            window(q, 0)
            window(q + 1, 1)
            quantize(q, 0)
            quantize(q + 1, 1)
            return c

        lax.fori_loop(0, ny // 2, two, 0)
        swap(k, x).start()

    def sum_cores(k):
        x = x_at(k)
        swap(k, x).wait_recv()

        def one(y, c):
            q = x * ny + y
            both = (qq[q, rows_of(mc), :].astype(F32) + from_core[q].astype(F32)).astype(BF16)
            s_a[x, y] = both[:, :hc]
            s_b[y, x] = both[:, hc:]
            return c

        lax.fori_loop(0, ny, one, 0)
        if k < nx:
            send_a(k).start()
        for j in range(1, ny):
            send_b(k, j).start()

    def send_a2(k):
        return remote(t_a.at[y_peer(k)], u_a.at[my], ya_s.at[k], ya_r.at[k], {"dp_1": y_peer(k)})

    def take_a2(k):
        return remote(t_a.at[0], u_a.at[y_source(k)], ya_s.at[k], ya_r.at[k], {"dp_1": y_peer(k)})

    def send_b2(k):
        return remote(t_b.at[x_peer(k)], u_b.at[mx], xb_s.at[k], xb_r.at[k], {"dp_0": x_peer(k)})

    def take_b2(k):
        return remote(t_b.at[0], u_b.at[x_source(k)], xb_s.at[k], xb_r.at[k], {"dp_0": x_peer(k)})

    def sum_b(k):
        x = x_at(k)
        for j in range(1, ny):
            take_b(k, j).wait_recv()
        so_far = s_b[my, x].astype(F32)
        for j in range(1, ny):
            so_far = so_far + r_b[y_source(j), x].astype(F32)
        t_b[x] = so_far.astype(BF16)
        if k < nx:
            send_b2(k).start()

    def add_a(y, c):
        so_far = s_a[mx, y].astype(F32)
        for k in range(1, nx):
            so_far = so_far + r_a[x_source(k), y].astype(F32)
        t_a[y] = so_far.astype(BF16)
        return c

    def sum_a():
        for k in range(1, nx):
            take_a(k).wait_recv()
        lax.fori_loop(0, ny, add_a, 0)
        for k in range(1, ny):
            send_a2(k).start()

    beside = [gain_second, gain_third, gain_fourth]
    for k in range(1, nx + 1):
        windows(k)
        if beside:
            beside.pop(0)()
        if k > 1:
            sum_cores(k - 1)
        if k > 2:
            sum_b(k - 2)
    sum_cores(nx)
    for job in beside:
        job()
    sum_b(nx - 1)
    sum_a()
    sum_b(nx)
    share = 1.0 / (nx * ny * 2)
    for k in range(1, ny):
        take_a2(k).wait_recv()
    so_far = t_a[my].astype(F32)
    for k in range(1, ny):
        so_far = so_far + u_a[y_source(k)].astype(F32)
    out[:, :hc] = so_far * share
    for k in range(1, nx):
        take_b2(k).wait_recv()
    so_far = t_b[mx].astype(F32)
    for k in range(1, nx):
        so_far = so_far + u_b[x_source(k)].astype(F32)
    out[:, hc:] = so_far * share

    def wait_gain(k, c):
        gain_z(k, z_source(k)).wait_recv()
        gain_z(k, mz).wait_send()
        send_rows(k).wait_send()
        send_sums(k, mz).wait_send()
        send_gz(k).wait_send()
        return c

    lax.fori_loop(1, nz, wait_gain, 0)
    for s in range(1, h + 1):
        for half in range(2):
            for flow in range(2):
                if in_ring(flow, s, half):
                    ring(flow, s, half).wait_send()
    for k in range(1, nx):
        w_x(k, mx).wait_send()
        gain_x(k, mx).wait_send()
        send_a(k).wait_send()
        send_b2(k).wait_send()
    for k in range(1, ny):
        w_y(k, my).wait_send()
        gain_y(k, my).wait_send()
        send_a2(k).wait_send()
    w_core(mc).wait_send()
    gain_core(mc).wait_send()
    for k in range(1, nx + 1):
        swap(k, x_at(k)).wait_send()
        for j in range(1, ny):
            send_b(k, j).wait_send()


def finish(ny, for_odd, for_core, summed, gain, weight_out, gain_out):
    odd = lax.rem(lax.axis_index("dp_1"), 2)
    at = odd * for_odd + lax.axis_index("dp_2") * for_core
    rows = summed.shape[0]
    weight_out[...] = pltpu.roll(summed[...], lax.rem(rows - at, rows), 0)[: weight_out.shape[0]]
    gain_out[...] = gain[...]


def on_device(
    sizes, tile_tokens, proj_weight, text_hidden, cotangent, norm_gain, placeholders, bucket_levels, row_draws, column_draws
):
    nx, ny, nz = sizes
    img_dev, vd = tile_tokens.shape[1:]
    own_rows, cols = proj_weight.shape
    tok, d = text_hidden.shape[1:]
    img = placeholders.shape[1]
    rows = up(own_rows, 16)
    win = up(2 * own_rows, 16)
    windows = nx * ny
    hc = cols // 2
    h = nz // 2
    dma = pltpu.SemaphoreType.DMA
    vmem = pl.BlockSpec(memory_space=pltpu.VMEM)
    scratch = [
        pltpu.VMEM((img, vd), BF16),
        pltpu.VMEM((vd, img), BF16),
        pltpu.VMEM((nx, ny, 2, rows, cols), BF16),
        pltpu.VMEM((vd, cols), BF16),
        pltpu.VMEM((tok, d), BF16),
        pltpu.VMEM((tok, d), BF16),
        pltpu.VMEM((nz, SLOTS, cols), BF16),
        pltpu.VMEM((nz * SLOTS, cols), BF16),
        pltpu.VMEM((img, cols), BF16),
        pltpu.VMEM((img, cols), BF16),
        pltpu.VMEM((img, cols), F32),
        pltpu.VMEM((img, nz * SLOTS), BF16),
        pltpu.VMEM((img, 128), F32),
        pltpu.VMEM((nz, 2, img), F32),
        pltpu.VMEM((tok, 128), F32),
        pltpu.VMEM((8, d), F32),
        pltpu.VMEM((nz, 1, cols), F32),
        pltpu.VMEM((nz, 1, cols), F32),
        pltpu.VMEM((2, 1, cols), F32),
        pltpu.VMEM((nx, 1, cols), F32),
        pltpu.VMEM((ny, 1, cols), F32),
        pltpu.VMEM((vd, 128), F32),
        pltpu.VMEM((windows, win, cols), BF16),
        pltpu.VMEM((windows, rows, cols), BF16),
        pltpu.VMEM((nx, ny, rows, hc), BF16),
        pltpu.VMEM((ny, nx, rows, hc), BF16),
        pltpu.VMEM((nx, ny, rows, hc), BF16),
        pltpu.VMEM((ny, nx, rows, hc), BF16),
        pltpu.VMEM((ny, rows, hc), BF16),
        pltpu.VMEM((nx, rows, hc), BF16),
        pltpu.VMEM((ny, rows, hc), BF16),
        pltpu.VMEM((nx, rows, hc), BF16),
        pltpu.VMEM((2, win, cols), F32),
        dma, dma,
        dma((2, h + 1, 2)), dma((2, h + 1, 2)),
        dma((nx,)), dma((nx,)), dma((ny,)), dma((ny,)), dma, dma,
        dma((nz,)), dma((nz,)), dma((nz,)), dma((nz,)), dma((nz,)), dma((nz,)),
        dma, dma, dma((nx,)), dma((nx,)), dma((ny,)), dma((ny,)), dma((nz,)), dma((nz,)),
        dma((nx + 1,)), dma((nx + 1,)),
        dma((nx,)), dma((nx,)), dma((ny,)), dma((ny,)), dma((nx + 1, ny)), dma((nx + 1, ny)), dma((nx,)), dma((nx,)),
    ]
    summed, gain_total = pl.pallas_call(
        functools.partial(kernel, sizes),
        out_shape=(
            jax.ShapeDtypeStruct((rows, cols), F32),
            jax.ShapeDtypeStruct((nz, 1, cols), F32),
        ),
        in_specs=[vmem] * 7 + [pl.BlockSpec(memory_space=pl.ANY)] * 2,
        out_specs=(vmem, vmem),
        scratch_shapes=scratch,
        compiler_params=pltpu.CompilerParams(
            collective_id=0, has_side_effects=True, vmem_limit_bytes=58 * 2**20
        ),
    )(
        tile_tokens[0],
        proj_weight,
        norm_gain.reshape(nz, 1, cols),
        placeholders,
        bucket_levels[0],
        row_draws[0],
        column_draws,
        cotangent[0],
        text_hidden[0],
    )
    weight, gain_grad = pl.pallas_call(
        functools.partial(finish, ny, win - 2 * own_rows, own_rows - (win - rows)),
        out_shape=(
            jax.ShapeDtypeStruct((own_rows, cols), F32),
            jax.ShapeDtypeStruct((nz, 1, cols), F32),
        ),
        in_specs=[vmem, vmem],
        out_specs=(vmem, vmem),
    )(summed, gain_total)
    return weight, gain_grad.reshape(d)


def solution(mesh):
    nz = mesh.shape["seq"]
    nx, ny = (4, 4) if mesh.shape["dp"] == 32 else (2, mesh.shape["dp"] // 4)
    finer = Mesh(mesh.devices.reshape(nx, ny, 2, nz), (*DP, "seq"))
    return jax.shard_map(
        functools.partial(on_device, (nx, ny, nz)),
        mesh=finer,
        in_specs=(
            P(DP, "seq", None),
            P(DP, "seq"),
            P(DP, "seq", None),
            P(DP, "seq", None),
            P(),
            P(DP, None),
            P(DP, "seq", None),
            P(DP, "seq", None),
            P(DP, "seq"),
        ),
        out_specs=(P(DP, "seq"), P()),
        check_vma=False,
    )
```

```python
import functools

import jax
import jax.numpy as jnp
from jax import lax
from jax.experimental import pallas as pl
from jax.experimental.pallas import tpu as pltpu
from jax.sharding import Mesh
from jax.sharding import PartitionSpec as P

DP = ("dp_0", "dp_1", "dp_2")
MESH = pl.DeviceIdType.MESH
EPSILON = 1e-06
SLOTS = 48
GROUP = 4
ORDER = (8, 1, 15, 7, 9, 2, 14, 6, 10, 3, 13, 5, 11, 4, 12)
ROWS_AT_STEP = (3, 2, 2, 2, 2, 2, 2, 0, 0)
F32 = jnp.float32
BF16 = jnp.bfloat16


def up(n, m):
    return -(-n // m) * m


def dot(a, b, dims=((1,), (0,))):
    return lax.dot_general(a, b, (dims, ((), ())), preferred_element_type=F32)


def iota(shape, axis):
    return lax.broadcasted_iota(jnp.int32, shape, axis)


def one_where(condition):
    return jnp.where(condition, 1.0, 0.0).astype(BF16)


def kernel(
    sizes,
    tile, w_own, gain, places, levels, row_draws, column_draws, cot_hbm, text_hbm,
    out, gain_out,
    tbuf, t_t, wbuf, wfull, cot, text, outb, inb, emb, eg, icot, picks, sm_c, smb, marks, gacc,
    gz, gz_in, g_core, g_x, g_y, meta, qq, from_core, s_a, s_b, r_a, r_b, t_a, t_b, u_a, u_b, grads,
    cot_sem, text_sem, ag_s, ag_r, wx_s, wx_r, wy_s, wy_r, wc_s, wc_r, a2a_s, a2a_r, sm_s, sm_r, gz_s, gz_r,
    gc_s, gc_r, gx_s, gx_r, gy_s, gy_r, gf_s, gf_r, qc_s, qc_r,
    xa_s, xa_r, ya_s, ya_r, yb_s, yb_r, xb_s, xb_r,
):
    nx, ny, nz = sizes
    own_rows, cols = w_own.shape
    rows = wbuf.shape[3]
    img_dev, vd = tile.shape
    half_rows = img_dev // 2
    img = tbuf.shape[0]
    tok, d = cot.shape
    win = qq.shape[1]
    hc = cols // 2
    h = nz // 2
    mx, my, mc, mz = (lax.axis_index(a) for a in ("dp_0", "dp_1", "dp_2", "seq"))
    oc = 1 - mc

    def z_peer(k):
        return {"seq": lax.rem(mz + k, nz)}

    def z_source(k):
        return lax.rem(mz + nz - k, nz)

    def x_peer(k):
        return lax.rem(mx + k, nx)

    def y_peer(k):
        return lax.rem(my + k, ny)

    def x_source(k):
        return lax.rem(mx + nx - k, nx)

    def y_source(k):
        return lax.rem(my + ny - k, ny)

    def remote(src, dst, send, recv, where):
        return pltpu.make_async_remote_copy(
            src_ref=src, dst_ref=dst, send_sem=send, recv_sem=recv, device_id=where, device_id_type=MESH
        )

    cot_copy = pltpu.make_async_copy(cot_hbm, cot, cot_sem)
    cot_copy.start()
    text_copy = pltpu.make_async_copy(text_hbm, text, text_sem)
    text_copy.start()

    barrier = pltpu.get_barrier_semaphore()

    def greet(where):
        pl.semaphore_signal(barrier, inc=1, device_id=where, device_id_type=MESH)

    def greet_z(k, c):
        greet(z_peer(k))
        return c

    lax.fori_loop(1, nz, greet_z, 0)
    for k in range(1, nx):
        greet({"dp_0": x_peer(k)})
    for k in range(1, ny):
        greet({"dp_1": y_peer(k)})
    greet({"dp_2": oc})

    tbuf[h * img_dev : (h + 1) * img_dev, :] = tile[...]
    same = iota((rows, own_rows), 0) == iota((rows, own_rows), 1)
    wbuf[mx, my, mc] = dot(one_where(same), w_own[...]).astype(BF16)
    base = mz * tok
    here = places[...]
    found = here == base + iota((tok, img), 0)
    marks[...] = jnp.broadcast_to(jnp.sum(jnp.where(found, 1.0, 0.0), axis=1, keepdims=True), marks.shape)
    start = jnp.sum(jnp.where(here < base, 1, 0), axis=1, keepdims=True)
    slot_of = one_where(iota((SLOTS, img), 1) - start == iota((SLOTS, img), 0))
    select = dot(slot_of, one_where(found), ((1,), (1,))).astype(BF16)

    pl.semaphore_wait(barrier, (nz - 1) + (nx - 1) + (ny - 1) + 1)

    def ring(flow, step, half):
        src_block = h - (step - 1) if flow == 0 else h + (step - 1)
        dst_block = (h - step if flow == 0 else h + step) % nz
        src = tbuf.at[pl.ds(src_block * img_dev + half * half_rows, half_rows)]
        dst = tbuf.at[pl.ds(dst_block * img_dev + half * half_rows, half_rows)]
        where = {"seq": lax.rem(mz + 1, nz) if flow == 0 else lax.rem(mz + nz - 1, nz)}
        return remote(src, dst, ag_s.at[flow, step, half], ag_r.at[flow, step, half], where)

    def in_ring(flow, step, half):
        return step < h or (step == h and half == flow)

    for half in range(2):
        for flow in range(2):
            if in_ring(flow, 1, half):
                ring(flow, 1, half).start()

    def ring_step(s):
        for half in range(2):
            for flow in range(2):
                if in_ring(flow, s, half):
                    ring(flow, s, half).wait_recv()
                    if in_ring(flow, s + 1, half):
                        ring(flow, s + 1, half).start()

    def w_x(k, slot):
        return remote(wbuf.at[slot, my, mc], wbuf.at[slot, my, mc], wx_s.at[k], wx_r.at[k], {"dp_0": x_peer(k)})

    def w_y(k, slot):
        return remote(wbuf.at[:, slot, mc], wbuf.at[:, slot, mc], wy_s.at[k], wy_r.at[k], {"dp_1": y_peer(k)})

    def w_core(slot):
        return remote(wbuf.at[:, :, slot], wbuf.at[:, :, slot], wc_s, wc_r, {"dp_2": oc})

    for k in range(1, nx):
        w_x(k, mx).start()

    def send_rows(k):
        to = lax.rem(mz + k, nz)
        return remote(
            outb.at[to], inb.at[pl.ds(pl.multiple_of(mz * SLOTS, 16), SLOTS)], a2a_s.at[k], a2a_r.at[k], z_peer(k)
        )

    def take_rows(k):
        return remote(
            outb.at[0], inb.at[pl.ds(pl.multiple_of(z_source(k) * SLOTS, 16), SLOTS)], a2a_s.at[k], a2a_r.at[k], z_peer(k)
        )

    def outgoing(z):
        at = pl.ds(pl.multiple_of(z * cols, 128), cols)
        return dot(select, cot[:, at]).astype(BF16)

    def pick(k):
        to = lax.rem(mz + k, nz)
        outb[to] = outgoing(to)
        send_rows(k).start()

    order = list(ORDER) if nz == 16 else list(range(1, nz))

    def pick_some(step):
        amount = ROWS_AT_STEP[step] if nz == 16 else nz
        for k in order[:amount]:
            pick(k)
        del order[:amount]

    cot_copy.wait()
    pick_some(0)
    inb[pl.ds(pl.multiple_of(mz * SLOTS, 16), SLOTS), :] = outgoing(mz)

    text_copy.wait()
    gacc[...] = jnp.zeros_like(gacc)

    def text_rows(i, c):
        at = pl.ds(pl.multiple_of(i * 16, 16), 16)
        squares = jnp.zeros((16, 1), F32)
        for z in range(nz):
            t = text[at, z * cols : (z + 1) * cols].astype(F32)
            squares += jnp.sum(t * t, axis=1, keepdims=True)
        inverse = jnp.where(marks[at, :1] > 0.5, 0.0, lax.rsqrt(squares / d + EPSILON))
        for z in range(nz):
            span = slice(z * cols, (z + 1) * cols)
            term = cot[at, span].astype(F32) * text[at, span].astype(F32) * inverse
            gacc[:, span] += term[:8] + term[8:]
        return c

    def text_part(first, last):
        lax.fori_loop(first, last, text_rows, 0)

    def send_gz(k):
        return remote(gz.at[lax.rem(mz + k, nz)], gz_in.at[mz], gz_s.at[k], gz_r.at[k], z_peer(k))

    def take_gz(k):
        return remote(gz.at[0], gz_in.at[z_source(k)], gz_s.at[k], gz_r.at[k], z_peer(k))

    def send_text_gain():
        for z in range(nz):
            gz[z] = jnp.sum(gacc[:, z * cols : (z + 1) * cols], axis=0, keepdims=True)

        def go(k, c):
            send_gz(k).start()
            return c

        lax.fori_loop(1, nz, go, 0)
        gz_in[mz] = gz[mz]

    def token_picks():
        slots = nz * SLOTS
        at = iota((1, slots), 1).astype(F32)
        owner = jnp.floor((at + 0.5) * (1.0 / SLOTS))
        placed = jnp.transpose(jnp.broadcast_to(here.astype(F32), (128, img)))[:, :1]
        first = jnp.sum(jnp.where(placed < owner * tok, 1.0, 0.0), axis=0, keepdims=True)
        last = jnp.sum(jnp.where(placed < owner * tok + tok, 1.0, 0.0), axis=0, keepdims=True)
        wanted = first + (at - owner * SLOTS)
        wanted = jnp.where(wanted < last, wanted, -1.0)
        for block in range(nz):
            shard = lax.rem(mz + nz - h + block, nz)
            token = (shard * img_dev + iota((img_dev, 1), 0)).astype(F32)
            picks[block * img_dev : (block + 1) * img_dev, :] = one_where(token == wanted)

    def bucket_columns():
        for at in range(0, vd, 128):
            n = min(128, vd - at)
            s = levels[:, at : at + n].astype(F32)
            r = 0.5 * row_draws[:, at : at + n]
            row = iota((128, n), 0)
            meta[at : at + n, :] = jnp.transpose(jnp.where(row == 0, s, jnp.where(row == 1, r, 1.0 / s)))

    def pack_projector():
        wide, packed = 4 * rows, 4 * own_rows
        i, j = iota((packed, wide), 0), iota((packed, wide), 1)
        shift = jnp.zeros((packed, wide), F32)
        for b in range(4):
            hit = (j - b * rows == i - b * own_rows) & (i >= b * own_rows) & (i < (b + 1) * own_rows)
            shift = jnp.where(hit, 1.0, shift)
        shift = shift.astype(BF16)

        def pack(g, c):
            x, y = g // (ny // 2), lax.rem(g, ny // 2) * 2
            block = wbuf[x, pl.ds(y, 2)].reshape(wide, cols)
            wfull[pl.ds(pl.multiple_of(g * packed, 16), packed), :] = dot(shift, block).astype(BF16)
            return c

        lax.fori_loop(0, nx * ny // 2, pack, 0)

    token_group = GROUP * img_dev

    def token_rows(g):
        at = slice(g * token_group, (g + 1) * token_group)
        rounded = dot(tbuf[at, :], wfull[...]).astype(BF16)
        emb[at, :] = rounded
        e = rounded.astype(F32)
        squares = jnp.sum(e * e, axis=1, keepdims=True)
        sm_c[at, :] = jnp.where(iota((token_group, 128), 1) == 0, squares, 0.0)

    def flip(g):
        at = slice(g * token_group, (g + 1) * token_group)
        for v in range(0, vd, 640):
            n = min(640, vd - v)
            t_t[v : v + n, at] = jnp.transpose(tbuf[at, v : v + n])

    groups = nz // GROUP
    done_at = [max(abs(GROUP * g - h), abs(GROUP * g + GROUP - 1 - h)) for g in range(groups)]

    plan = {s: [] for s in range(1, h + 1)}

    def at_step(s, job):
        plan[min(max(s, 1), h)].append(job)

    def w_second():
        for k in range(1, nx):
            w_x(k, x_source(k)).wait_recv()
        for k in range(1, ny):
            w_y(k, my).start()

    def w_third():
        for k in range(1, ny):
            w_y(k, y_source(k)).wait_recv()
        w_core(mc).start()

    def w_last():
        w_core(oc).wait_recv()
        pack_projector()

    row_chunks = tok // 16
    w_done = min(5, h)
    at_step(1, lambda: text_part(0, row_chunks // 2))
    at_step(1, w_second)
    at_step(2, lambda: text_part(row_chunks // 2, row_chunks))
    at_step(2, send_text_gain)
    at_step(3, w_third)
    at_step(3, bucket_columns)
    at_step(min(4, h - 1), token_picks)
    at_step(w_done, w_last)
    for g in sorted(range(groups), key=lambda g: done_at[g]):
        at_step(max(done_at[g], w_done), functools.partial(token_rows, g))
        if done_at[g] < h - 1:
            at_step(done_at[g], functools.partial(flip, g))

    def wait_rows(k, c):
        take_rows(k).wait_recv()
        return c

    own_gain = gain[mz]

    def pick_group(g, c):
        at = pl.ds(pl.multiple_of(g * token_group, token_group), token_group)
        icot[at, :] = dot(picks[at, :], inb[...])
        return c

    def pick_arrived():
        lax.fori_loop(1, nz, wait_rows, 0)
        lax.fori_loop(0, groups, pick_group, 0)

    def token_products(g):
        def some(i, c):
            at = pl.ds(pl.multiple_of(g * token_group + i * 32, 32), 32)
            mixed = jnp.sum(icot[at, :] * own_gain * emb[at, :].astype(F32), axis=1, keepdims=True)
            sm_c[at, :] = jnp.where(iota((32, 128), 1) == 1, mixed, sm_c[at, :])
            return c

        lax.fori_loop(0, token_group // 32, some, 0, unroll=True)

    early = [g for g in range(groups) if done_at[g] < h]
    late = [g for g in range(groups) if done_at[g] >= h]
    for s in range(1, h + 1):
        if s == h and not order:
            pick_arrived()
            for g in early:
                token_products(g)
        ring_step(s)
        if order:
            pick_some(s)
        for job in plan[s]:
            job()
    for g in late:
        token_products(g)

    turn = img_dev * lax.rem(mz + nz - h, nz)
    turn_back = img_dev * lax.rem(h + nz - mz, nz)
    smb[mz] = pltpu.roll(jnp.transpose(sm_c[...])[:8], turn, 1)[:2]

    def send_sums(k, source):
        return remote(smb.at[source], smb.at[source], sm_s.at[k], sm_r.at[k], z_peer(k))

    def wait_gz(k, c):
        take_gz(k).wait_recv()
        return c

    def wait_sums(k, c):
        send_sums(k, z_source(k)).wait_recv()
        return c

    for k in sorted(range(1, nz), key=lambda k: -min(k, nz - k)):
        send_sums(k, mz).start()
    for g in range(groups):
        if done_at[g] >= h - 1:
            flip(g)
    lax.fori_loop(1, nz, wait_gz, 0)
    text_gain = gz_in[0]
    for z in range(1, nz):
        text_gain = text_gain + gz_in[z]
    lax.fori_loop(1, nz, wait_sums, 0)
    total = smb[0]
    for z in range(1, nz):
        total = total + smb[z]
    total = pltpu.roll(jnp.concatenate([total] * 4, axis=0), turn_back, 1)
    inverse = lax.rsqrt(total[0:1] / d + EPSILON)
    factor = total[1:2] * inverse / d * inverse
    row = iota((128, img), 0)
    sm_c[...] = jnp.transpose(jnp.where(row == 0, inverse, jnp.where(row == 1, factor, 0.0)))

    def token_grads(g, part):
        first = pl.multiple_of(g * token_group, token_group)
        for i in range(0, token_group, 16):
            at = pl.ds(first + i, 16)
            e = emb[at, :].astype(F32)
            ic = icot[at, :]
            inv, fac = sm_c[at, 0:1], sm_c[at, 1:2]
            eg[at, :] = ((ic * own_gain - e * fac) * inv).astype(BF16)
            term = ic * e * inv
            part = part + term[:8] + term[8:]
        return part

    part = lax.fori_loop(0, groups, token_grads, jnp.zeros((8, cols), F32))
    part = jnp.sum(part, axis=0, keepdims=True)

    g_core[mc] = part + text_gain

    def gain_core(slot):
        return remote(g_core.at[slot], g_core.at[slot], gc_s, gc_r, {"dp_2": oc})

    def gain_x(k, slot):
        return remote(g_x.at[slot], g_x.at[slot], gx_s.at[k], gx_r.at[k], {"dp_0": x_peer(k)})

    def gain_y(k, slot):
        return remote(g_y.at[slot], g_y.at[slot], gy_s.at[k], gy_r.at[k], {"dp_1": y_peer(k)})

    def gain_z(k, slot):
        return remote(gain_out.at[slot], gain_out.at[slot], gf_s.at[k], gf_r.at[k], z_peer(k))

    gain_core(mc).start()

    def gain_second():
        gain_core(oc).wait_recv()
        g_x[mx] = g_core[0] + g_core[1]
        for k in range(1, nx):
            gain_x(k, mx).start()

    def gain_third():
        for k in range(1, nx):
            gain_x(k, x_source(k)).wait_recv()
        so_far = g_x[0]
        for x in range(1, nx):
            so_far = so_far + g_x[x]
        g_y[my] = so_far
        for k in range(1, ny):
            gain_y(k, my).start()

    def gain_fourth():
        for k in range(1, ny):
            gain_y(k, y_source(k)).wait_recv()
        so_far = g_y[0]
        for y in range(1, ny):
            so_far = so_far + g_y[y]
        gain_out[mz] = so_far * (1.0 / (nx * ny * 2))

        def go(k, c):
            gain_z(k, mz).start()
            return c

        lax.fori_loop(1, nz, go, 0)

    column_part = 0.5 * column_draws[...]

    def first_row(q):
        return pl.multiple_of(2 * own_rows * q - 8 * lax.rem(q, 2), 8)

    def window(q, slot):
        grads[slot] = dot(t_t[pl.ds(pl.multiple_of(first_row(q), 16), win), :], eg[...])

    def quantize(q, slot):
        for i in range(0, win, 16):
            grad = grads[slot, i : i + 16, :]
            at = pl.ds(first_row(q) + i, 16)
            square = jnp.sum(grad * grad, axis=1, keepdims=True) + EPSILON
            root = lax.rsqrt(square)
            s, r, s_inverse = meta[at, 0:1], meta[at, 1:2], meta[at, 2:3]
            ratio = jnp.abs(grad) * (s * root)
            lower = jnp.floor(ratio)
            quantum = lower + jnp.clip(2.0 * (ratio - lower) - (r + column_part), 0.0, 1.0)
            size = quantum * (square * root * s_inverse)
            value = jnp.where(grad < 0.0, -size, size).astype(BF16)
            qq[q, i : i + 16, :] = value

    def rows_of(core):
        return pl.ds(pl.multiple_of(core * (win - rows), 16), rows)

    def y_at(j):
        return lax.rem(my + j, ny)

    def swap(k, j):
        q = x_at(k) * ny + y_at(j)
        return remote(qq.at[q, rows_of(oc)], from_core.at[q], qc_s.at[k, j], qc_r.at[k, j], {"dp_2": oc})

    def send_a(k, j):
        y = y_at(j)
        return remote(s_a.at[x_at(k), y], r_a.at[mx, y], xa_s.at[k, j], xa_r.at[k, j], {"dp_0": x_peer(k)})

    def take_a(k, j):
        y = y_at(j)
        return remote(s_a.at[0, y], r_a.at[x_source(k), y], xa_s.at[k, j], xa_r.at[k, j], {"dp_0": x_peer(k)})

    def send_b(k, j):
        x = x_at(k)
        return remote(s_b.at[y_peer(j), x], r_b.at[my, x], yb_s.at[k, j], yb_r.at[k, j], {"dp_1": y_peer(j)})

    def take_b(k, j):
        x = x_at(k)
        return remote(s_b.at[0, x], r_b.at[y_source(j), x], yb_s.at[k, j], yb_r.at[k, j], {"dp_1": y_peer(j)})

    def x_at(k):
        return lax.rem(mx + k, nx)

    def sum_cores(k, j):
        x, y = x_at(k), y_at(j)
        q = x * ny + y
        swap(k, j).wait_recv()
        both = (qq[q, rows_of(mc), :].astype(F32) + from_core[q].astype(F32)).astype(BF16)
        s_a[x, y] = both[:, :hc]
        s_b[y, x] = both[:, hc:]

        @pl.when(k < nx)
        def to_x():
            send_a(k, j).start()

        @pl.when(j < ny)
        def to_y():
            send_b(k, j).start()

    def send_a2(k):
        return remote(t_a.at[y_peer(k)], u_a.at[my], ya_s.at[k], ya_r.at[k], {"dp_1": y_peer(k)})

    def take_a2(k):
        return remote(t_a.at[0], u_a.at[y_source(k)], ya_s.at[k], ya_r.at[k], {"dp_1": y_peer(k)})

    def send_b2(k):
        return remote(t_b.at[x_peer(k)], u_b.at[mx], xb_s.at[k], xb_r.at[k], {"dp_0": x_peer(k)})

    def take_b2(k):
        return remote(t_b.at[0], u_b.at[x_source(k)], xb_s.at[k], xb_r.at[k], {"dp_0": x_peer(k)})

    def sum_b(k):
        x = x_at(k)
        for j in range(1, ny):
            take_b(k, j).wait_recv()
        so_far = s_b[my, x].astype(F32)
        for j in range(1, ny):
            so_far = so_far + r_b[y_source(j), x].astype(F32)
        t_b[x] = so_far.astype(BF16)

    def sum_a(j):
        y = y_at(j)
        for k in range(1, nx):
            take_a(k, j).wait_recv()
        so_far = s_a[mx, y].astype(F32)
        for k in range(1, nx):
            so_far = so_far + r_a[x_source(k), y].astype(F32)
        t_a[y] = so_far.astype(BF16)

    pairs = ny // 2
    steps = nx * pairs
    beside = {1: gain_second, 2: gain_third, 3: gain_fourth}

    def pair_of(t):
        return 1 + t // pairs, 2 * lax.rem(t, pairs) + 1

    def step_pair(t, c):
        k, j = pair_of(t)
        base_q = x_at(k) * ny
        window(base_q + y_at(j), 0)
        window(base_q + y_at(j + 1), 1)
        quantize(base_q + y_at(j), 0)
        swap(k, j).start()
        quantize(base_q + y_at(j + 1), 1)
        swap(k, j + 1).start()
        for at, job in beside.items():
            pl.when(t == at * pairs - 1)(job)

        @pl.when(t > 0)
        def before():
            k_last, j_last = pair_of(t - 1)
            sum_cores(k_last, j_last)
            sum_cores(k_last, j_last + 1)

        @pl.when((t >= 3 * pairs - 1) & (lax.rem(t, pairs) == pairs - 1))
        def second():
            sum_b(k - 2)
            send_b2(k - 2).start()

        return c

    lax.fori_loop(0, steps, step_pair, 0)
    sum_cores(nx, ny - 1)
    sum_cores(nx, ny)
    sum_b(nx - 1)
    if nx > 1:
        send_b2(nx - 1).start()
    for j in range(1, ny + 1):
        sum_a(j)
        if j < ny:
            send_a2(j).start()
    sum_b(nx)
    share = 1.0 / (nx * ny * 2)
    for k in range(1, ny):
        take_a2(k).wait_recv()
    so_far = t_a[my].astype(F32)
    for k in range(1, ny):
        so_far = so_far + u_a[y_source(k)].astype(F32)
    out[:, :hc] = so_far * share
    for k in range(1, nx):
        take_b2(k).wait_recv()
    so_far = t_b[mx].astype(F32)
    for k in range(1, nx):
        so_far = so_far + u_b[x_source(k)].astype(F32)
    out[:, hc:] = so_far * share

    def wait_gain(k, c):
        gain_z(k, z_source(k)).wait_recv()
        gain_z(k, mz).wait_send()
        send_rows(k).wait_send()
        send_sums(k, mz).wait_send()
        send_gz(k).wait_send()
        return c

    lax.fori_loop(1, nz, wait_gain, 0)
    for s in range(1, h + 1):
        for half in range(2):
            for flow in range(2):
                if in_ring(flow, s, half):
                    ring(flow, s, half).wait_send()
    for k in range(1, nx):
        w_x(k, mx).wait_send()
        gain_x(k, mx).wait_send()
        for j in range(1, ny + 1):
            send_a(k, j).wait_send()
        send_b2(k).wait_send()
    for k in range(1, ny):
        w_y(k, my).wait_send()
        gain_y(k, my).wait_send()
        send_a2(k).wait_send()
    w_core(mc).wait_send()
    gain_core(mc).wait_send()
    for k in range(1, nx + 1):
        for j in range(1, ny + 1):
            swap(k, j).wait_send()
        for j in range(1, ny):
            send_b(k, j).wait_send()


def finish(ny, for_odd, for_core, summed, gain, weight_out, gain_out):
    odd = lax.rem(lax.axis_index("dp_1"), 2)
    at = odd * for_odd + lax.axis_index("dp_2") * for_core
    rows = summed.shape[0]
    weight_out[...] = pltpu.roll(summed[...], lax.rem(rows - at, rows), 0)[: weight_out.shape[0]]
    gain_out[...] = gain[...]


def on_device(
    sizes, tile_tokens, proj_weight, text_hidden, cotangent, norm_gain, placeholders, bucket_levels, row_draws, column_draws
):
    nx, ny, nz = sizes
    img_dev, vd = tile_tokens.shape[1:]
    own_rows, cols = proj_weight.shape
    tok, d = text_hidden.shape[1:]
    img = placeholders.shape[1]
    rows = up(own_rows, 16)
    win = up(2 * own_rows, 16)
    windows = nx * ny
    hc = cols // 2
    h = nz // 2
    dma = pltpu.SemaphoreType.DMA
    vmem = pl.BlockSpec(memory_space=pltpu.VMEM)
    scratch = [
        pltpu.VMEM((img, vd), BF16),
        pltpu.VMEM((vd, img), BF16),
        pltpu.VMEM((nx, ny, 2, rows, cols), BF16),
        pltpu.VMEM((vd, cols), BF16),
        pltpu.VMEM((tok, d), BF16),
        pltpu.VMEM((tok, d), BF16),
        pltpu.VMEM((nz, SLOTS, cols), BF16),
        pltpu.VMEM((nz * SLOTS, cols), BF16),
        pltpu.VMEM((img, cols), BF16),
        pltpu.VMEM((img, cols), BF16),
        pltpu.VMEM((img, cols), F32),
        pltpu.VMEM((img, nz * SLOTS), BF16),
        pltpu.VMEM((img, 128), F32),
        pltpu.VMEM((nz, 2, img), F32),
        pltpu.VMEM((tok, 128), F32),
        pltpu.VMEM((8, d), F32),
        pltpu.VMEM((nz, 1, cols), F32),
        pltpu.VMEM((nz, 1, cols), F32),
        pltpu.VMEM((2, 1, cols), F32),
        pltpu.VMEM((nx, 1, cols), F32),
        pltpu.VMEM((ny, 1, cols), F32),
        pltpu.VMEM((vd, 128), F32),
        pltpu.VMEM((windows, win, cols), BF16),
        pltpu.VMEM((windows, rows, cols), BF16),
        pltpu.VMEM((nx, ny, rows, hc), BF16),
        pltpu.VMEM((ny, nx, rows, hc), BF16),
        pltpu.VMEM((nx, ny, rows, hc), BF16),
        pltpu.VMEM((ny, nx, rows, hc), BF16),
        pltpu.VMEM((ny, rows, hc), BF16),
        pltpu.VMEM((nx, rows, hc), BF16),
        pltpu.VMEM((ny, rows, hc), BF16),
        pltpu.VMEM((nx, rows, hc), BF16),
        pltpu.VMEM((2, win, cols), F32),
        dma, dma,
        dma((2, h + 1, 2)), dma((2, h + 1, 2)),
        dma((nx,)), dma((nx,)), dma((ny,)), dma((ny,)), dma, dma,
        dma((nz,)), dma((nz,)), dma((nz,)), dma((nz,)), dma((nz,)), dma((nz,)),
        dma, dma, dma((nx,)), dma((nx,)), dma((ny,)), dma((ny,)), dma((nz,)), dma((nz,)),
        dma((nx + 1, ny + 1)), dma((nx + 1, ny + 1)),
        dma((nx, ny + 1)), dma((nx, ny + 1)), dma((ny,)), dma((ny,)), dma((nx + 1, ny)), dma((nx + 1, ny)), dma((nx,)), dma((nx,)),
    ]
    summed, gain_total = pl.pallas_call(
        functools.partial(kernel, sizes),
        out_shape=(
            jax.ShapeDtypeStruct((rows, cols), F32),
            jax.ShapeDtypeStruct((nz, 1, cols), F32),
        ),
        in_specs=[vmem] * 7 + [pl.BlockSpec(memory_space=pl.ANY)] * 2,
        out_specs=(vmem, vmem),
        scratch_shapes=scratch,
        compiler_params=pltpu.CompilerParams(
            collective_id=0, has_side_effects=True, vmem_limit_bytes=58 * 2**20
        ),
    )(
        tile_tokens[0],
        proj_weight,
        norm_gain.reshape(nz, 1, cols),
        placeholders,
        bucket_levels[0],
        row_draws[0],
        column_draws,
        cotangent[0],
        text_hidden[0],
    )
    weight, gain_grad = pl.pallas_call(
        functools.partial(finish, ny, win - 2 * own_rows, own_rows - (win - rows)),
        out_shape=(
            jax.ShapeDtypeStruct((own_rows, cols), F32),
            jax.ShapeDtypeStruct((nz, 1, cols), F32),
        ),
        in_specs=[vmem, vmem],
        out_specs=(vmem, vmem),
    )(summed, gain_total)
    return weight, gain_grad.reshape(d)


def solution(mesh):
    nz = mesh.shape["seq"]
    nx, ny = (4, 4) if mesh.shape["dp"] == 32 else (2, mesh.shape["dp"] // 4)
    finer = Mesh(mesh.devices.reshape(nx, ny, 2, nz), (*DP, "seq"))
    return jax.shard_map(
        functools.partial(on_device, (nx, ny, nz)),
        mesh=finer,
        in_specs=(
            P(DP, "seq", None),
            P(DP, "seq"),
            P(DP, "seq", None),
            P(DP, "seq", None),
            P(),
            P(DP, None),
            P(DP, "seq", None),
            P(DP, "seq", None),
            P(DP, "seq"),
        ),
        out_specs=(P(DP, "seq"), P()),
        check_vma=False,
    )
```

```python
import functools

import jax
import jax.numpy as jnp
from jax import lax
from jax.experimental import pallas as pl
from jax.experimental.pallas import tpu as pltpu
from jax.sharding import Mesh
from jax.sharding import PartitionSpec as P

DP = ("dp_0", "dp_1", "dp_2")
MESH = pl.DeviceIdType.MESH
EPSILON = 1e-06
SLOTS = 48
GROUP = 4
ORDER = (8, 1, 15, 7, 9, 2, 14, 6, 10, 3, 13, 5, 11, 4, 12)
ROWS_AT_STEP = (3, 2, 2, 2, 2, 2, 2, 0, 0)
F32 = jnp.float32
BF16 = jnp.bfloat16


def up(n, m):
    return -(-n // m) * m


def dot(a, b, dims=((1,), (0,))):
    return lax.dot_general(a, b, (dims, ((), ())), preferred_element_type=F32)


def iota(shape, axis):
    return lax.broadcasted_iota(jnp.int32, shape, axis)


def one_where(condition):
    return jnp.where(condition, 1.0, 0.0).astype(BF16)


def kernel(
    sizes,
    tile, w_own, gain, places, levels, row_draws, column_draws, cot_hbm, text_hbm,
    out, gain_out,
    tbuf, t_t, wbuf, wfull, cot, text, outb, inb, emb, eg, icot, picks, sm_c, smb, marks, gacc,
    gz, gz_in, g_core, g_x, g_y, meta, qq, from_core, s_a, s_b, r_a, r_b, t_a, t_b, u_a, u_b, grads,
    cot_sem, text_sem, ag_s, ag_r, wx_s, wx_r, wy_s, wy_r, wc_s, wc_r, a2a_s, a2a_r, sm_s, sm_r, gz_s, gz_r,
    gc_s, gc_r, gx_s, gx_r, gy_s, gy_r, gf_s, gf_r, qc_s, qc_r,
    xa_s, xa_r, ya_s, ya_r, yb_s, yb_r, xb_s, xb_r,
):
    nx, ny, nz = sizes
    own_rows, cols = w_own.shape
    rows = wbuf.shape[3]
    img_dev, vd = tile.shape
    half_rows = img_dev // 2
    img = tbuf.shape[0]
    tok, d = cot.shape
    win = qq.shape[1]
    hc = cols // 2
    h = nz // 2
    mx, my, mc, mz = (lax.axis_index(a) for a in ("dp_0", "dp_1", "dp_2", "seq"))
    oc = 1 - mc

    def z_peer(k):
        return {"seq": lax.rem(mz + k, nz)}

    def z_source(k):
        return lax.rem(mz + nz - k, nz)

    def x_peer(k):
        return lax.rem(mx + k, nx)

    def y_peer(k):
        return lax.rem(my + k, ny)

    def x_source(k):
        return lax.rem(mx + nx - k, nx)

    def y_source(k):
        return lax.rem(my + ny - k, ny)

    def remote(src, dst, send, recv, where):
        return pltpu.make_async_remote_copy(
            src_ref=src, dst_ref=dst, send_sem=send, recv_sem=recv, device_id=where, device_id_type=MESH
        )

    cot_copy = pltpu.make_async_copy(cot_hbm, cot, cot_sem)
    cot_copy.start()
    text_copy = pltpu.make_async_copy(text_hbm, text, text_sem)
    text_copy.start()

    barrier = pltpu.get_barrier_semaphore()

    def greet(where):
        pl.semaphore_signal(barrier, inc=1, device_id=where, device_id_type=MESH)

    def greet_z(k, c):
        greet(z_peer(k))
        return c

    lax.fori_loop(1, nz, greet_z, 0)
    for k in range(1, nx):
        greet({"dp_0": x_peer(k)})
    for k in range(1, ny):
        greet({"dp_1": y_peer(k)})
    greet({"dp_2": oc})

    tbuf[h * img_dev : (h + 1) * img_dev, :] = tile[...]
    same = iota((rows, own_rows), 0) == iota((rows, own_rows), 1)
    wbuf[mx, my, mc] = dot(one_where(same), w_own[...]).astype(BF16)
    base = mz * tok
    here = places[...]
    found = here == base + iota((tok, img), 0)
    marks[...] = jnp.broadcast_to(jnp.sum(jnp.where(found, 1.0, 0.0), axis=1, keepdims=True), marks.shape)
    start = jnp.sum(jnp.where(here < base, 1, 0), axis=1, keepdims=True)
    slot_of = one_where(iota((SLOTS, img), 1) - start == iota((SLOTS, img), 0))
    select = dot(slot_of, one_where(found), ((1,), (1,))).astype(BF16)

    pl.semaphore_wait(barrier, (nz - 1) + (nx - 1) + (ny - 1) + 1)

    def ring(flow, step, half):
        src_block = h - (step - 1) if flow == 0 else h + (step - 1)
        dst_block = (h - step if flow == 0 else h + step) % nz
        src = tbuf.at[pl.ds(src_block * img_dev + half * half_rows, half_rows)]
        dst = tbuf.at[pl.ds(dst_block * img_dev + half * half_rows, half_rows)]
        where = {"seq": lax.rem(mz + 1, nz) if flow == 0 else lax.rem(mz + nz - 1, nz)}
        return remote(src, dst, ag_s.at[flow, step, half], ag_r.at[flow, step, half], where)

    def in_ring(flow, step, half):
        return step < h or (step == h and half == flow)

    for half in range(2):
        for flow in range(2):
            if in_ring(flow, 1, half):
                ring(flow, 1, half).start()

    def ring_step(s):
        for half in range(2):
            for flow in range(2):
                if in_ring(flow, s, half):
                    ring(flow, s, half).wait_recv()
                    if in_ring(flow, s + 1, half):
                        ring(flow, s + 1, half).start()

    def w_x(k, slot):
        return remote(wbuf.at[slot, my, mc], wbuf.at[slot, my, mc], wx_s.at[k], wx_r.at[k], {"dp_0": x_peer(k)})

    def w_y(k, slot):
        return remote(wbuf.at[:, slot, mc], wbuf.at[:, slot, mc], wy_s.at[k], wy_r.at[k], {"dp_1": y_peer(k)})

    def w_core(slot):
        return remote(wbuf.at[:, :, slot], wbuf.at[:, :, slot], wc_s, wc_r, {"dp_2": oc})

    for k in range(1, nx):
        w_x(k, mx).start()

    def send_rows(k):
        to = lax.rem(mz + k, nz)
        return remote(
            outb.at[to], inb.at[pl.ds(pl.multiple_of(mz * SLOTS, 16), SLOTS)], a2a_s.at[k], a2a_r.at[k], z_peer(k)
        )

    def take_rows(k):
        return remote(
            outb.at[0], inb.at[pl.ds(pl.multiple_of(z_source(k) * SLOTS, 16), SLOTS)], a2a_s.at[k], a2a_r.at[k], z_peer(k)
        )

    def outgoing(z):
        at = pl.ds(pl.multiple_of(z * cols, 128), cols)
        return dot(select, cot[:, at]).astype(BF16)

    def pick(k):
        to = lax.rem(mz + k, nz)
        outb[to] = outgoing(to)
        send_rows(k).start()

    order = list(ORDER) if nz == 16 else list(range(1, nz))

    def pick_some(step):
        amount = ROWS_AT_STEP[step] if nz == 16 else nz
        for k in order[:amount]:
            pick(k)
        del order[:amount]

    cot_copy.wait()
    pick_some(0)
    inb[pl.ds(pl.multiple_of(mz * SLOTS, 16), SLOTS), :] = outgoing(mz)

    text_copy.wait()
    gacc[...] = jnp.zeros_like(gacc)

    def text_rows(i, c):
        at = pl.ds(pl.multiple_of(i * 16, 16), 16)
        squares = jnp.zeros((16, 1), F32)
        for z in range(nz):
            t = text[at, z * cols : (z + 1) * cols].astype(F32)
            squares += jnp.sum(t * t, axis=1, keepdims=True)
        inverse = jnp.where(marks[at, :1] > 0.5, 0.0, lax.rsqrt(squares / d + EPSILON))
        for z in range(nz):
            span = slice(z * cols, (z + 1) * cols)
            term = cot[at, span].astype(F32) * text[at, span].astype(F32) * inverse
            gacc[:, span] += term[:8] + term[8:]
        return c

    def text_part(first, last):
        lax.fori_loop(first, last, text_rows, 0)

    def send_gz(k):
        return remote(gz.at[lax.rem(mz + k, nz)], gz_in.at[mz], gz_s.at[k], gz_r.at[k], z_peer(k))

    def take_gz(k):
        return remote(gz.at[0], gz_in.at[z_source(k)], gz_s.at[k], gz_r.at[k], z_peer(k))

    def send_text_gain():
        for z in range(nz):
            gz[z] = jnp.sum(gacc[:, z * cols : (z + 1) * cols], axis=0, keepdims=True)

        def go(k, c):
            send_gz(k).start()
            return c

        lax.fori_loop(1, nz, go, 0)
        gz_in[mz] = gz[mz]

    def token_picks():
        slots = nz * SLOTS
        at = iota((1, slots), 1).astype(F32)
        owner = jnp.floor((at + 0.5) * (1.0 / SLOTS))
        placed = jnp.transpose(jnp.broadcast_to(here.astype(F32), (128, img)))[:, :1]
        first = jnp.sum(jnp.where(placed < owner * tok, 1.0, 0.0), axis=0, keepdims=True)
        last = jnp.sum(jnp.where(placed < owner * tok + tok, 1.0, 0.0), axis=0, keepdims=True)
        wanted = first + (at - owner * SLOTS)
        wanted = jnp.where(wanted < last, wanted, -1.0)
        for block in range(nz):
            shard = lax.rem(mz + nz - h + block, nz)
            token = (shard * img_dev + iota((img_dev, 1), 0)).astype(F32)
            picks[block * img_dev : (block + 1) * img_dev, :] = one_where(token == wanted)

    def bucket_columns():
        for at in range(0, vd, 128):
            n = min(128, vd - at)
            s = levels[:, at : at + n].astype(F32)
            r = 0.5 * row_draws[:, at : at + n]
            row = iota((128, n), 0)
            meta[at : at + n, :] = jnp.transpose(jnp.where(row == 0, s, jnp.where(row == 1, r, 1.0 / s)))

    def pack_projector():
        wide, packed = 4 * rows, 4 * own_rows
        i, j = iota((packed, wide), 0), iota((packed, wide), 1)
        shift = jnp.zeros((packed, wide), F32)
        for b in range(4):
            hit = (j - b * rows == i - b * own_rows) & (i >= b * own_rows) & (i < (b + 1) * own_rows)
            shift = jnp.where(hit, 1.0, shift)
        shift = shift.astype(BF16)

        def pack(g, c):
            x, y = g // (ny // 2), lax.rem(g, ny // 2) * 2
            block = wbuf[x, pl.ds(y, 2)].reshape(wide, cols)
            wfull[pl.ds(pl.multiple_of(g * packed, 16), packed), :] = dot(shift, block).astype(BF16)
            return c

        lax.fori_loop(0, nx * ny // 2, pack, 0)

    token_group = GROUP * img_dev

    def token_rows(g):
        at = slice(g * token_group, (g + 1) * token_group)
        rounded = dot(tbuf[at, :], wfull[...]).astype(BF16)
        emb[at, :] = rounded
        e = rounded.astype(F32)
        squares = jnp.sum(e * e, axis=1, keepdims=True)
        sm_c[at, :] = jnp.where(iota((token_group, 128), 1) == 0, squares, 0.0)

    def flip(g):
        at = slice(g * token_group, (g + 1) * token_group)
        for v in range(0, vd, 640):
            n = min(640, vd - v)
            t_t[v : v + n, at] = jnp.transpose(tbuf[at, v : v + n])

    groups = nz // GROUP
    done_at = [max(abs(GROUP * g - h), abs(GROUP * g + GROUP - 1 - h)) for g in range(groups)]

    plan = {s: [] for s in range(1, h + 1)}

    def at_step(s, job):
        plan[min(max(s, 1), h)].append(job)

    def w_second():
        for k in range(1, nx):
            w_x(k, x_source(k)).wait_recv()
        for k in range(1, ny):
            w_y(k, my).start()

    def w_third():
        for k in range(1, ny):
            w_y(k, y_source(k)).wait_recv()
        w_core(mc).start()

    def w_last():
        w_core(oc).wait_recv()
        pack_projector()

    row_chunks = tok // 16
    w_done = min(5, h)
    for i in range(4):
        at_step(1 + i, functools.partial(text_part, row_chunks * i // 4, row_chunks * (i + 1) // 4))
    at_step(1, w_second)
    at_step(4, send_text_gain)
    at_step(3, w_third)
    at_step(6, bucket_columns)
    at_step(min(3, h - 1), token_picks)
    at_step(w_done, w_last)
    for g in sorted(range(groups), key=lambda g: done_at[g]):
        at_step(max(done_at[g], w_done), functools.partial(token_rows, g))
        if done_at[g] < h - 1:
            at_step(done_at[g], functools.partial(flip, g))

    def wait_rows(k, c):
        take_rows(k).wait_recv()
        return c

    own_gain = gain[mz]

    def pick_group(g, c):
        at = pl.ds(pl.multiple_of(g * token_group, token_group), token_group)
        icot[at, :] = dot(picks[at, :], inb[...])
        return c

    def pick_arrived():
        lax.fori_loop(1, nz, wait_rows, 0)
        lax.fori_loop(0, groups, pick_group, 0)

    def token_products(g):
        def some(i, c):
            at = pl.ds(pl.multiple_of(g * token_group + i * 32, 32), 32)
            mixed = jnp.sum(icot[at, :] * own_gain * emb[at, :].astype(F32), axis=1, keepdims=True)
            sm_c[at, :] = jnp.where(iota((32, 128), 1) == 1, mixed, sm_c[at, :])
            return c

        lax.fori_loop(0, token_group // 32, some, 0, unroll=True)

    early = [g for g in range(groups) if done_at[g] < h]
    late = [g for g in range(groups) if done_at[g] >= h]
    for s in range(1, h + 1):
        if s == h and not order:
            pick_arrived()
            for g in early:
                token_products(g)
        ring_step(s)
        if order:
            pick_some(s)
        for job in plan[s]:
            job()
    for g in late:
        token_products(g)

    turn = img_dev * lax.rem(mz + nz - h, nz)
    turn_back = img_dev * lax.rem(h + nz - mz, nz)
    smb[mz] = pltpu.roll(jnp.transpose(sm_c[...])[:8], turn, 1)[:2]

    def send_sums(k, source):
        return remote(smb.at[source], smb.at[source], sm_s.at[k], sm_r.at[k], z_peer(k))

    def wait_gz(k, c):
        take_gz(k).wait_recv()
        return c

    def wait_sums(k, c):
        send_sums(k, z_source(k)).wait_recv()
        return c

    for k in sorted(range(1, nz), key=lambda k: -min(k, nz - k)):
        send_sums(k, mz).start()
    for g in range(groups):
        if done_at[g] >= h - 1:
            flip(g)
    lax.fori_loop(1, nz, wait_gz, 0)
    text_gain = gz_in[0]
    for z in range(1, nz):
        text_gain = text_gain + gz_in[z]
    lax.fori_loop(1, nz, wait_sums, 0)
    total = smb[0]
    for z in range(1, nz):
        total = total + smb[z]
    total = pltpu.roll(jnp.concatenate([total] * 4, axis=0), turn_back, 1)
    inverse = lax.rsqrt(total[0:1] / d + EPSILON)
    factor = total[1:2] * inverse / d * inverse
    row = iota((128, img), 0)
    sm_c[...] = jnp.transpose(jnp.where(row == 0, inverse, jnp.where(row == 1, factor, 0.0)))

    def token_grads(g, part):
        first = pl.multiple_of(g * token_group, token_group)
        for i in range(0, token_group, 16):
            at = pl.ds(first + i, 16)
            e = emb[at, :].astype(F32)
            ic = icot[at, :]
            inv, fac = sm_c[at, 0:1], sm_c[at, 1:2]
            eg[at, :] = ((ic * own_gain - e * fac) * inv).astype(BF16)
            term = ic * e * inv
            part = part + term[:8] + term[8:]
        return part

    part = lax.fori_loop(0, groups, token_grads, jnp.zeros((8, cols), F32))
    part = jnp.sum(part, axis=0, keepdims=True)

    g_core[mc] = part + text_gain

    def gain_core(slot):
        return remote(g_core.at[slot], g_core.at[slot], gc_s, gc_r, {"dp_2": oc})

    def gain_x(k, slot):
        return remote(g_x.at[slot], g_x.at[slot], gx_s.at[k], gx_r.at[k], {"dp_0": x_peer(k)})

    def gain_y(k, slot):
        return remote(g_y.at[slot], g_y.at[slot], gy_s.at[k], gy_r.at[k], {"dp_1": y_peer(k)})

    def gain_z(k, slot):
        return remote(gain_out.at[slot], gain_out.at[slot], gf_s.at[k], gf_r.at[k], z_peer(k))

    gain_core(mc).start()

    def gain_second():
        gain_core(oc).wait_recv()
        g_x[mx] = g_core[0] + g_core[1]
        for k in range(1, nx):
            gain_x(k, mx).start()

    def gain_third():
        for k in range(1, nx):
            gain_x(k, x_source(k)).wait_recv()
        so_far = g_x[0]
        for x in range(1, nx):
            so_far = so_far + g_x[x]
        g_y[my] = so_far
        for k in range(1, ny):
            gain_y(k, my).start()

    def gain_fourth():
        for k in range(1, ny):
            gain_y(k, y_source(k)).wait_recv()
        so_far = g_y[0]
        for y in range(1, ny):
            so_far = so_far + g_y[y]
        gain_out[mz] = so_far * (1.0 / (nx * ny * 2))

        def go(k, c):
            gain_z(k, mz).start()
            return c

        lax.fori_loop(1, nz, go, 0)

    column_part = 0.5 * column_draws[...]

    def first_row(q):
        return pl.multiple_of(2 * own_rows * q - 8 * lax.rem(q, 2), 8)

    def window(q, slot):
        grads[slot] = dot(t_t[pl.ds(pl.multiple_of(first_row(q), 16), win), :], eg[...])

    def quantize(q, slot):
        for i in range(0, win, 16):
            grad = grads[slot, i : i + 16, :]
            at = pl.ds(first_row(q) + i, 16)
            square = jnp.sum(grad * grad, axis=1, keepdims=True) + EPSILON
            root = lax.rsqrt(square)
            s, r, s_inverse = meta[at, 0:1], meta[at, 1:2], meta[at, 2:3]
            ratio = jnp.abs(grad) * (s * root)
            lower = jnp.floor(ratio)
            quantum = lower + jnp.clip(2.0 * (ratio - lower) - (r + column_part), 0.0, 1.0)
            size = quantum * (square * root * s_inverse)
            value = jnp.where(grad < 0.0, -size, size).astype(BF16)
            qq[q, i : i + 16, :] = value

    def rows_of(core):
        return pl.ds(pl.multiple_of(core * (win - rows), 16), rows)

    def y_at(j):
        return lax.rem(my + j, ny)

    def swap(k, j):
        q = x_at(k) * ny + y_at(j)
        return remote(qq.at[q, rows_of(oc)], from_core.at[q], qc_s.at[k, j], qc_r.at[k, j], {"dp_2": oc})

    def send_a(k, j):
        y = y_at(j)
        return remote(s_a.at[x_at(k), y], r_a.at[mx, y], xa_s.at[k, j], xa_r.at[k, j], {"dp_0": x_peer(k)})

    def take_a(k, j):
        y = y_at(j)
        return remote(s_a.at[0, y], r_a.at[x_source(k), y], xa_s.at[k, j], xa_r.at[k, j], {"dp_0": x_peer(k)})

    def send_b(k, j):
        x = x_at(k)
        return remote(s_b.at[y_peer(j), x], r_b.at[my, x], yb_s.at[k, j], yb_r.at[k, j], {"dp_1": y_peer(j)})

    def take_b(k, j):
        x = x_at(k)
        return remote(s_b.at[0, x], r_b.at[y_source(j), x], yb_s.at[k, j], yb_r.at[k, j], {"dp_1": y_peer(j)})

    def x_at(k):
        return lax.rem(mx + k, nx)

    def sum_cores(k, j):
        x, y = x_at(k), y_at(j)
        q = x * ny + y
        swap(k, j).wait_recv()
        both = (qq[q, rows_of(mc), :].astype(F32) + from_core[q].astype(F32)).astype(BF16)
        s_a[x, y] = both[:, :hc]
        s_b[y, x] = both[:, hc:]

        @pl.when(k < nx)
        def to_x():
            send_a(k, j).start()

        @pl.when(j < ny)
        def to_y():
            send_b(k, j).start()

    def send_a2(k):
        return remote(t_a.at[y_peer(k)], u_a.at[my], ya_s.at[k], ya_r.at[k], {"dp_1": y_peer(k)})

    def take_a2(k):
        return remote(t_a.at[0], u_a.at[y_source(k)], ya_s.at[k], ya_r.at[k], {"dp_1": y_peer(k)})

    def send_b2(k):
        return remote(t_b.at[x_peer(k)], u_b.at[mx], xb_s.at[k], xb_r.at[k], {"dp_0": x_peer(k)})

    def take_b2(k):
        return remote(t_b.at[0], u_b.at[x_source(k)], xb_s.at[k], xb_r.at[k], {"dp_0": x_peer(k)})

    def sum_b(k):
        x = x_at(k)
        for j in range(1, ny):
            take_b(k, j).wait_recv()
        so_far = s_b[my, x].astype(F32)
        for j in range(1, ny):
            so_far = so_far + r_b[y_source(j), x].astype(F32)
        t_b[x] = so_far.astype(BF16)

    def sum_a(j):
        y = y_at(j)
        for k in range(1, nx):
            take_a(k, j).wait_recv()
        so_far = s_a[mx, y].astype(F32)
        for k in range(1, nx):
            so_far = so_far + r_a[x_source(k), y].astype(F32)
        t_a[y] = so_far.astype(BF16)

    pairs = ny // 2
    steps = nx * pairs
    beside = ((1, gain_second), (2, gain_third), (3, gain_fourth))

    def pair_of(t):
        return 1 + t // pairs, 2 * lax.rem(t, pairs) + 1

    def step_pair(t, c):
        k, j = pair_of(t)
        base_q = x_at(k) * ny
        window(base_q + y_at(j), 0)
        window(base_q + y_at(j + 1), 1)
        quantize(base_q + y_at(j), 0)
        swap(k, j).start()
        quantize(base_q + y_at(j + 1), 1)
        swap(k, j + 1).start()
        for at, job in beside:
            pl.when(t == min(at * pairs, steps) - 1)(job)

        @pl.when(t > 0)
        def before():
            k_last, j_last = pair_of(t - 1)
            sum_cores(k_last, j_last)
            sum_cores(k_last, j_last + 1)

        @pl.when((t >= 3 * pairs - 1) & (lax.rem(t, pairs) == pairs - 1))
        def second():
            sum_b(k - 2)
            send_b2(k - 2).start()

        return c

    lax.fori_loop(0, steps, step_pair, 0)
    sum_cores(nx, ny - 1)
    sum_cores(nx, ny)
    sum_b(nx - 1)
    if nx > 1:
        send_b2(nx - 1).start()
    for j in range(1, ny + 1):
        sum_a(j)
        if j < ny:
            send_a2(j).start()
    sum_b(nx)
    share = 1.0 / (nx * ny * 2)
    for k in range(1, ny):
        take_a2(k).wait_recv()
    so_far = t_a[my].astype(F32)
    for k in range(1, ny):
        so_far = so_far + u_a[y_source(k)].astype(F32)
    out[:, :hc] = so_far * share
    for k in range(1, nx):
        take_b2(k).wait_recv()
    so_far = t_b[mx].astype(F32)
    for k in range(1, nx):
        so_far = so_far + u_b[x_source(k)].astype(F32)
    out[:, hc:] = so_far * share

    def wait_gain(k, c):
        gain_z(k, z_source(k)).wait_recv()
        gain_z(k, mz).wait_send()
        send_rows(k).wait_send()
        send_sums(k, mz).wait_send()
        send_gz(k).wait_send()
        return c

    lax.fori_loop(1, nz, wait_gain, 0)
    for s in range(1, h + 1):
        for half in range(2):
            for flow in range(2):
                if in_ring(flow, s, half):
                    ring(flow, s, half).wait_send()
    for k in range(1, nx):
        w_x(k, mx).wait_send()
        gain_x(k, mx).wait_send()
        for j in range(1, ny + 1):
            send_a(k, j).wait_send()
        send_b2(k).wait_send()
    for k in range(1, ny):
        w_y(k, my).wait_send()
        gain_y(k, my).wait_send()
        send_a2(k).wait_send()
    w_core(mc).wait_send()
    gain_core(mc).wait_send()
    for k in range(1, nx + 1):
        for j in range(1, ny + 1):
            swap(k, j).wait_send()
        for j in range(1, ny):
            send_b(k, j).wait_send()


def finish(ny, for_odd, for_core, summed, gain, weight_out, gain_out):
    odd = lax.rem(lax.axis_index("dp_1"), 2)
    at = odd * for_odd + lax.axis_index("dp_2") * for_core
    rows = summed.shape[0]
    weight_out[...] = pltpu.roll(summed[...], lax.rem(rows - at, rows), 0)[: weight_out.shape[0]]
    gain_out[...] = gain[...]


def on_device(
    sizes, tile_tokens, proj_weight, text_hidden, cotangent, norm_gain, placeholders, bucket_levels, row_draws, column_draws
):
    nx, ny, nz = sizes
    img_dev, vd = tile_tokens.shape[1:]
    own_rows, cols = proj_weight.shape
    tok, d = text_hidden.shape[1:]
    img = placeholders.shape[1]
    rows = up(own_rows, 16)
    win = up(2 * own_rows, 16)
    windows = nx * ny
    hc = cols // 2
    h = nz // 2
    dma = pltpu.SemaphoreType.DMA
    vmem = pl.BlockSpec(memory_space=pltpu.VMEM)
    scratch = [
        pltpu.VMEM((img, vd), BF16),
        pltpu.VMEM((vd, img), BF16),
        pltpu.VMEM((nx, ny, 2, rows, cols), BF16),
        pltpu.VMEM((vd, cols), BF16),
        pltpu.VMEM((tok, d), BF16),
        pltpu.VMEM((tok, d), BF16),
        pltpu.VMEM((nz, SLOTS, cols), BF16),
        pltpu.VMEM((nz * SLOTS, cols), BF16),
        pltpu.VMEM((img, cols), BF16),
        pltpu.VMEM((img, cols), BF16),
        pltpu.VMEM((img, cols), F32),
        pltpu.VMEM((img, nz * SLOTS), BF16),
        pltpu.VMEM((img, 128), F32),
        pltpu.VMEM((nz, 2, img), F32),
        pltpu.VMEM((tok, 128), F32),
        pltpu.VMEM((8, d), F32),
        pltpu.VMEM((nz, 1, cols), F32),
        pltpu.VMEM((nz, 1, cols), F32),
        pltpu.VMEM((2, 1, cols), F32),
        pltpu.VMEM((nx, 1, cols), F32),
        pltpu.VMEM((ny, 1, cols), F32),
        pltpu.VMEM((vd, 128), F32),
        pltpu.VMEM((windows, win, cols), BF16),
        pltpu.VMEM((windows, rows, cols), BF16),
        pltpu.VMEM((nx, ny, rows, hc), BF16),
        pltpu.VMEM((ny, nx, rows, hc), BF16),
        pltpu.VMEM((nx, ny, rows, hc), BF16),
        pltpu.VMEM((ny, nx, rows, hc), BF16),
        pltpu.VMEM((ny, rows, hc), BF16),
        pltpu.VMEM((nx, rows, hc), BF16),
        pltpu.VMEM((ny, rows, hc), BF16),
        pltpu.VMEM((nx, rows, hc), BF16),
        pltpu.VMEM((2, win, cols), F32),
        dma, dma,
        dma((2, h + 1, 2)), dma((2, h + 1, 2)),
        dma((nx,)), dma((nx,)), dma((ny,)), dma((ny,)), dma, dma,
        dma((nz,)), dma((nz,)), dma((nz,)), dma((nz,)), dma((nz,)), dma((nz,)),
        dma, dma, dma((nx,)), dma((nx,)), dma((ny,)), dma((ny,)), dma((nz,)), dma((nz,)),
        dma((nx + 1, ny + 1)), dma((nx + 1, ny + 1)),
        dma((nx, ny + 1)), dma((nx, ny + 1)), dma((ny,)), dma((ny,)), dma((nx + 1, ny)), dma((nx + 1, ny)), dma((nx,)), dma((nx,)),
    ]
    summed, gain_total = pl.pallas_call(
        functools.partial(kernel, sizes),
        out_shape=(
            jax.ShapeDtypeStruct((rows, cols), F32),
            jax.ShapeDtypeStruct((nz, 1, cols), F32),
        ),
        in_specs=[vmem] * 7 + [pl.BlockSpec(memory_space=pl.ANY)] * 2,
        out_specs=(vmem, vmem),
        scratch_shapes=scratch,
        compiler_params=pltpu.CompilerParams(
            collective_id=0, has_side_effects=True, vmem_limit_bytes=58 * 2**20
        ),
    )(
        tile_tokens[0],
        proj_weight,
        norm_gain.reshape(nz, 1, cols),
        placeholders,
        bucket_levels[0],
        row_draws[0],
        column_draws,
        cotangent[0],
        text_hidden[0],
    )
    weight, gain_grad = pl.pallas_call(
        functools.partial(finish, ny, win - 2 * own_rows, own_rows - (win - rows)),
        out_shape=(
            jax.ShapeDtypeStruct((own_rows, cols), F32),
            jax.ShapeDtypeStruct((nz, 1, cols), F32),
        ),
        in_specs=[vmem, vmem],
        out_specs=(vmem, vmem),
    )(summed, gain_total)
    return weight, gain_grad.reshape(d)


def solution(mesh):
    nz = mesh.shape["seq"]
    nx, ny = (4, 4) if mesh.shape["dp"] == 32 else (2, mesh.shape["dp"] // 4)
    finer = Mesh(mesh.devices.reshape(nx, ny, 2, nz), (*DP, "seq"))
    return jax.shard_map(
        functools.partial(on_device, (nx, ny, nz)),
        mesh=finer,
        in_specs=(
            P(DP, "seq", None),
            P(DP, "seq"),
            P(DP, "seq", None),
            P(DP, "seq", None),
            P(),
            P(DP, None),
            P(DP, "seq", None),
            P(DP, "seq", None),
            P(DP, "seq"),
        ),
        out_specs=(P(DP, "seq"), P()),
        check_vma=False,
    )
```
